32 devices in a mesh: dp: 8 (over z, y), ctx: 4 (over x, core).
Axes of the slice: x: 2, y: 2, z: 4, core: 2. Of those that a mesh axis runs over, the one named last changes fastest.
Arguments:
- tokens: bfloat16 [2, 2048, 896], P(None, ('dp', 'ctx')), may hold values from -6 to 6
- seq_lengths: int32 [8, 2, 3], P('dp'), may hold values from 1 to 254, as said below
- attn_params: bfloat16 [1839104], P(('dp', 'ctx'))
- ffn_weight: bfloat16 [3, 4864, 896], P(None, ('dp', 'ctx'))
- out_grad: bfloat16 [2, 2048, 896], P(None, ('dp', 'ctx')), may hold values from -6 to 6
Outputs:
- output: bfloat16 [2, 2048, 896], P(None, ('dp', 'ctx'))
- input_grad: bfloat16 [2, 2048, 896], P(None, ('dp', 'ctx'))
- attn_grad: float32 [1839104], P(('dp', 'ctx'))
- ffn_grad: float32 [3, 4864, 896], P(None, ('dp', 'ctx'))
The draws below stay inside these ranges and needn't reach their ends.
Inputs may be any that keep to these rules, and one draw needn't show every extreme that they name: seq_lengths[g, m, :] are the lengths of 3 sequences packed in order from slot 0 of stream g of micro-batch m; their sum is at most 256, the other slots are padding.
All inputs are finite; a program needn't handle non-finite values.
Results may differ from the reference program's by a relative error of at most 0.013.
Values may be sent and summed in bfloat16 or wider, within the bound.
A program may use at most 256 MiB of HBM per device.

```python
import math
import jax
import jax.numpy as jnp
from jax import lax

D = 896
HEADS = 14
KV_HEADS = 2
HEAD = 64
FF = 4864
BLOCK = 64
MB = 2
STREAM = 256
TOKENS = 2048
ATT_PAD = 1839104
N_DP = 8


def draw_seq_lengths(key, part):
    key = jax.random.fold_in(key, 5)
    key_short, key_long, key_place = jax.random.split(key, 3)
    half_block = BLOCK // 2
    shorts = jax.random.randint(key_short, (N_DP, MB, 2), 1, half_block)
    room = STREAM - jnp.sum(shorts, axis=-1)
    longest = jax.random.randint(key_long, (N_DP, MB), STREAM - BLOCK + 1, room + 1)
    place = jax.random.randint(key_place, (N_DP, MB), 0, 3)
    first_len = jnp.where(place == 0, longest, shorts[..., 0])
    middle_len = jnp.where(place == 0, shorts[..., 0], jnp.where(place == 1, longest, shorts[..., 1]))
    last_len = jnp.where(place == 2, longest, shorts[..., 1])
    lengths = jnp.stack([first_len, middle_len, last_len], axis=-1).astype(jnp.int32)
    lengths = lengths.at[0, 0].set(jnp.array([STREAM - 2, 1, 1], jnp.int32))
    return lengths


def draw_attn_params(key, part):
    key = jax.random.fold_in(key, 11)
    kv_width = KV_HEADS * HEAD
    counts_list = [D * D, D * kv_width, D * kv_width, D * D, D, kv_width, kv_width, D, D]
    scales_list = [D ** (-0.5), D ** (-0.5), D ** (-0.5), 6.0 * D ** (-0.5), 0.3, 0.5, 0.3, 0.0, 0.0]
    indices = jnp.arange(ATT_PAD, dtype=jnp.int32)
    noise = jax.random.normal(key, (ATT_PAD,), jnp.float32)
    gains = jax.random.uniform(jax.random.fold_in(key, 1), (ATT_PAD,), jnp.float32, 0.6, 1.4)
    scale_vec = jnp.full((ATT_PAD,), 0.02, jnp.float32)
    offset = 0
    for entries, factor in zip(counts_list, scales_list):
        inside = (indices >= offset) & (indices < offset + entries)
        scale_vec = jnp.where(inside, factor, scale_vec)
        offset += entries
    gain_start = offset - 2 * D
    in_gain = (indices >= gain_start) & (indices < offset)
    return jnp.where(in_gain, gains, noise * scale_vec).astype(jnp.bfloat16)


def draw_ffn_weight(key, part):
    key = jax.random.fold_in(key, 7)
    noise = jax.random.normal(key, (3, FF, D), jnp.float32)
    scale_vec = jnp.array([D ** (-0.5), D ** (-0.5), 1.5 * FF ** (-0.5)], jnp.float32)
    return (noise * scale_vec[:, None, None]).astype(jnp.bfloat16)


def level_of(own_key, shape, cuts, least, top_value):
    loudness = 1.0
    for axis_at, shards_of in cuts:
        heights = jax.random.uniform(jax.random.fold_in(jax.random.fold_in(own_key, 6), axis_at), (shards_of,), jnp.float32, least / len(cuts), top_value / len(cuts))
        loudness = loudness * jnp.repeat(jnp.exp(heights), shape[axis_at] // shards_of).reshape((-1,) + (1,) * (len(shape) - 1 - axis_at))
    return loudness


def gaussian(key, extent, deviation, most, cuts=(), held_as=jnp.bfloat16):
    factor_of = level_of(key, extent, cuts, -0.22, 0.18) if cuts else 1.0
    values = jax.random.normal(key, extent, jnp.float32) * deviation * factor_of
    return jnp.minimum(jnp.maximum(values, -most), most).astype(held_as)


def setup_inputs(seed: int = 0) -> dict:
    keys = jax.random.split(jax.random.key(seed), 6)
    tokens = gaussian(keys[0], (MB, TOKENS, D), 1.0, 6.0, ((1, 32),))
    seq_lengths = draw_seq_lengths(jax.random.fold_in(keys[5], 71), 0)
    attn_params = draw_attn_params(jax.random.fold_in(keys[5], 71), 0)
    ffn_weight = draw_ffn_weight(jax.random.fold_in(keys[5], 71), 0)
    out_grad = gaussian(keys[4], (MB, TOKENS, D), 1.0, 6.0, ((1, 32),))
    return {"tokens": tokens, "seq_lengths": seq_lengths, "attn_params": attn_params, "ffn_weight": ffn_weight, "out_grad": out_grad}


EPSILON = 1e-06
THETA = 1000000.0

@jax.custom_vjp
def low(v):
    return lax.optimization_barrier(v.astype(jnp.bfloat16)).astype(jnp.float32)

@jax.custom_vjp
def low_back(v):
    return v

def low_keep(v):
    return (low(v), None)

def low_pass(kept, grad):
    return (grad,)

def back_keep(v):
    return (v, None)

def back_low(kept, grad):
    return (low(grad),)
low.defvjp(low_keep, low_pass)
low_back.defvjp(back_keep, back_low)

def matmul_high(left, right):
    return jnp.dot(left, right, precision=lax.Precision.HIGHEST)

def rms_norm(values, gain_vec):
    return values * lax.rsqrt(lax.optimization_barrier(jnp.mean(values * values, axis=-1, keepdims=True)) + EPSILON) * gain_vec

def rotate(values, cosine, sine_table):
    half_width = values.shape[-1] // 2
    turned = jnp.concatenate([-values[..., half_width:], values[..., :half_width]], axis=-1)
    return values * cosine + turned * sine_table

def geometry(seq_lens, slot_ids):
    seq_ends = jnp.cumsum(seq_lens).astype(jnp.int32)
    seq_starts = (seq_ends - seq_lens).astype(jnp.int32)
    filled = seq_ends[-1]
    numbers = jnp.arange(seq_lens.shape[0], dtype=jnp.int32)
    segment = lax.optimization_barrier(jnp.sum((slot_ids[:, None] >= seq_ends[None, :]).astype(jnp.int32), axis=1)).astype(jnp.int32)
    seq_begin = lax.optimization_barrier(jnp.sum(jnp.where(segment[:, None] == numbers[None, :], seq_starts[None, :], 0), axis=1)).astype(jnp.int32)
    inside = slot_ids < filled
    segment = jnp.where(inside, segment, seq_lens.shape[0] + slot_ids).astype(jnp.int32)
    position = jnp.where(inside, slot_ids - seq_begin, 0).astype(jnp.int32)
    return (segment, position)

def rotary_tables(position):
    half_width = HEAD // 2
    frequency = jnp.power(THETA, -(jnp.arange(half_width, dtype=jnp.float32) * 2.0 / HEAD))
    angles = position.astype(jnp.float32)[:, None] * frequency[None, :]
    cosine = jnp.concatenate([jnp.cos(angles), jnp.cos(angles)], axis=-1)
    sine_table = jnp.concatenate([jnp.sin(angles), jnp.sin(angles)], axis=-1)
    return (cosine, sine_table)

def unpack(flat_params):
    kv_width = KV_HEADS * HEAD
    shapes_list = [(D, D), (D, kv_width), (D, kv_width), (D, D), (D,), (kv_width,), (kv_width,), (D,), (D,)]
    pieces = []
    offset = 0
    for piece_shape in shapes_list:
        entries = math.prod(piece_shape)
        pieces.append(flat_params[offset:offset + entries].reshape(piece_shape))
        offset += entries
    return pieces

def forward(flat_params, ffn_params, stream_in, seq_lens):
    w_query, w_key, w_value, w_out, b_query, b_key, b_value, gain_one, gain_two = unpack(flat_params)
    rows_all = stream_in.shape[0]
    score_scale = HEAD ** (-0.5)
    slot_ids = jnp.arange(rows_all, dtype=jnp.int32)
    segment, position = geometry(seq_lens, slot_ids)
    cosine, sine_table = rotary_tables(position)
    cos_heads = cosine[:, None, :]
    sin_heads = sine_table[:, None, :]
    normed = low(rms_norm(stream_in, gain_one))
    query_pre = low_back(matmul_high(normed, w_query) + b_query).reshape(rows_all, HEADS, HEAD)
    query = low(rotate(query_pre, cos_heads, sin_heads)).reshape(rows_all, KV_HEADS, HEADS // KV_HEADS, HEAD)
    key_pre = low_back(matmul_high(normed, w_key) + b_key).reshape(rows_all, KV_HEADS, HEAD)
    key_rot = low(rotate(key_pre, cos_heads, sin_heads))
    value_low = low(low_back(matmul_high(normed, w_value) + b_value)).reshape(rows_all, KV_HEADS, HEAD)
    scores = low_back(jnp.einsum('qkgd,skd->kgqs', query, key_rot, precision=lax.Precision.HIGHEST) * score_scale)
    allowed = (segment[:, None] == segment[None, :]) & (slot_ids[None, :] <= slot_ids[:, None])
    scores = jnp.where(allowed[None, None], scores, -1e+30)
    probs = low(jax.nn.softmax(scores, axis=-1))
    mixed = jnp.einsum('kgqs,skd->qkgd', probs, value_low, precision=lax.Precision.HIGHEST).reshape(rows_all, HEADS * HEAD)
    mixed = low(low_back(mixed))
    second = stream_in + low_back(matmul_high(mixed, w_out))
    normed_two = low(rms_norm(second, gain_two))
    gate_out = low_back(jnp.einsum('td,fd->tf', normed_two, ffn_params[0], precision=lax.Precision.HIGHEST))
    up_out = low_back(jnp.einsum('td,fd->tf', normed_two, ffn_params[1], precision=lax.Precision.HIGHEST))
    hidden = low(jax.nn.silu(gate_out) * up_out)
    return second + jnp.einsum('tf,fd->td', hidden, ffn_params[2], precision=lax.Precision.HIGHEST)

def reference(tokens, seq_lengths, attn_params, ffn_weight, out_grad):
    flat_params = attn_params.astype(jnp.float32)
    ffn_params = ffn_weight.astype(jnp.float32)
    micro_count = tokens.shape[0]
    width = tokens.shape[2]
    stream = tokens.shape[1] // N_DP
    inputs = tokens.astype(jnp.float32).reshape(micro_count, N_DP, stream, width).transpose(1, 0, 2, 3)
    cotangents = out_grad.astype(jnp.float32).reshape(micro_count, N_DP, stream, width).transpose(1, 0, 2, 3)

    def step(carry, stream_item):
        stream_in, stream_cot, seq_lens = stream_item

        def forward_all(flat_p, ffn_p, values):
            return jax.vmap(lambda single, lens_one: forward(flat_p, ffn_p, single, lens_one))(values, seq_lens)
        result, pullback = jax.vjp(forward_all, flat_params, ffn_params, stream_in)
        grad_flat, grad_ffn, grad_in = pullback(stream_cot)
        return ((carry[0] + grad_flat, carry[1] + grad_ffn), (result, grad_in))
    zero_grads = (jnp.zeros(flat_params.shape, jnp.float32), jnp.zeros(ffn_params.shape, jnp.float32))
    (grad_flat, grad_ffn), (results, grad_ins) = lax.scan(step, zero_grads, (inputs, cotangents, seq_lengths))
    output = results.transpose(1, 0, 2, 3).reshape(micro_count, N_DP * stream, width)
    input_grad = grad_ins.transpose(1, 0, 2, 3).reshape(micro_count, N_DP * stream, width)
    return (output.astype(jnp.bfloat16), input_grad.astype(jnp.bfloat16), grad_flat, grad_ffn)
```

```python
import math

import jax
import jax.numpy as jnp
from jax import lax
from jax.sharding import Mesh
from jax.sharding import PartitionSpec as P

D = 896
HEADS = 14
KV_HEADS = 2
HEAD = 64


EPSILON = 1e-06
THETA = 1000000.0


def rms_norm(values, gain_vec):
    return (
        values * lax.rsqrt(jnp.mean(values * values, axis=-1, keepdims=True) + EPSILON) * gain_vec
    )


def rotate(values, cosine, sine_table):
    half_width = values.shape[-1] // 2
    turned = jnp.concatenate([-values[..., half_width:], values[..., :half_width]], axis=-1)
    return values * cosine + turned * sine_table


def rotate_back(incoming, cosine, sine_table):
    scaled = incoming * sine_table
    half_width = incoming.shape[-1] // 2
    turned = jnp.concatenate([scaled[..., half_width:], -scaled[..., :half_width]], axis=-1)
    return incoming * cosine + turned


def geometry(seq_lens, slot_ids):
    seq_ends = jnp.cumsum(seq_lens)
    seq_starts = seq_ends - seq_lens
    filled = seq_ends[-1]
    numbers = jnp.arange(seq_lens.shape[0], dtype=jnp.int32)
    segment = jnp.sum((slot_ids[:, None] >= seq_ends[None, :]).astype(jnp.int32), axis=1)
    seq_begin = jnp.sum(
        jnp.where(segment[:, None] == numbers[None, :], seq_starts[None, :], 0), axis=1
    )
    inside = slot_ids < filled
    segment = jnp.where(inside, segment, seq_lens.shape[0] + slot_ids)
    position = jnp.where(inside, slot_ids - seq_begin, 0)
    return (segment, position)


def rotary_tables(position):
    half_width = HEAD // 2
    frequency = jnp.power(THETA, -(jnp.arange(half_width, dtype=jnp.float32) * 2.0 / HEAD))
    angles = position.astype(jnp.float32)[:, None] * frequency[None, :]
    cosine = jnp.concatenate([jnp.cos(angles), jnp.cos(angles)], axis=-1)
    sine_table = jnp.concatenate([jnp.sin(angles), jnp.sin(angles)], axis=-1)
    return (cosine, sine_table)


def unpack(flat_params):
    kv_width = KV_HEADS * HEAD
    shapes_list = [
        (D, D),
        (D, kv_width),
        (D, kv_width),
        (D, D),
        (D,),
        (kv_width,),
        (kv_width,),
        (D,),
        (D,),
    ]
    pieces = []
    offset = 0
    for piece_shape in shapes_list:
        entries = math.prod(piece_shape)
        pieces.append(flat_params[offset : offset + entries].reshape(piece_shape))
        offset += entries
    return pieces


def pack_grads(pieces, total_length):
    flat_grad = jnp.concatenate([piece.reshape(-1) for piece in pieces])
    padding = total_length - flat_grad.shape[0]
    return jnp.concatenate([flat_grad, jnp.zeros((padding,), jnp.float32)])


def per_device(tokens, seq_lengths, attn_params, ffn_weight, out_grad):
    micro_count, rows_own = tokens.shape[0], tokens.shape[1]
    stream = rows_own * lax.axis_size("ctx")
    rows = micro_count * rows_own
    groups = HEADS // KV_HEADS
    kv_width = KV_HEADS * HEAD
    score_scale = HEAD ** (-0.5)
    units = ffn_weight.shape[1]
    far = lax.axis_size("hi")
    devices = far * lax.axis_size("lo") * lax.axis_size("ctx")
    total_length = attn_params.shape[0] * devices
    f32, bf16 = jnp.float32, jnp.bfloat16

    cot_low = out_grad.reshape(rows, D)
    ffn_all = lax.all_gather(ffn_weight.reshape(3 * units, D), "hi", axis=0, tiled=False)
    attn_all = lax.all_gather(
        attn_params.reshape(-1, 128), ("hi", "lo", "ctx"), axis=0, tiled=False
    ).reshape(-1)
    cot_all = lax.all_gather(cot_low, ("lo", "ctx"), axis=0, tiled=True)
    w_query, w_key, w_value, w_out, b_query, b_key, b_value, gain_one, gain_two = unpack(attn_all)
    w_qkv = jnp.concatenate([w_query, w_key, w_value], axis=1)
    b_qkv = jnp.concatenate([b_query, b_key, b_value], axis=0).astype(f32)

    slot_ids = jnp.arange(stream, dtype=jnp.int32)
    first_slot = lax.axis_index("ctx") * rows_own
    own_slots = first_slot + jnp.arange(rows_own, dtype=jnp.int32)
    segment, position = jax.vmap(geometry, in_axes=(0, None))(seq_lengths[0], slot_ids)
    own_segment = lax.dynamic_slice_in_dim(segment, first_slot, rows_own, axis=1)
    own_position = lax.dynamic_slice_in_dim(position, first_slot, rows_own, axis=1)
    cosine, sine_table = rotary_tables(own_position.reshape(-1))
    cos_heads, sin_heads = cosine[:, None, :], sine_table[:, None, :]
    allowed = (own_segment[:, :, None] == segment[:, None, :]) & (
        slot_ids[None, None, :] <= own_slots[None, :, None]
    )

    x_float = tokens.reshape(rows, D).astype(f32)
    normed, norm_pull = jax.vjp(rms_norm, x_float, gain_one.astype(f32))
    normed_low = normed.astype(bf16)
    qkv = jnp.dot(normed_low, w_qkv, preferred_element_type=f32) + b_qkv
    query_pre, key_pre, value_pre = jnp.split(qkv, [D, D + kv_width], axis=1)
    query_low = rotate(query_pre.reshape(rows, HEADS, HEAD), cos_heads, sin_heads).astype(bf16)
    key_low = rotate(key_pre.reshape(rows, KV_HEADS, HEAD), cos_heads, sin_heads).astype(bf16)
    kv_low = jnp.concatenate([key_low.reshape(rows, kv_width), value_pre.astype(bf16)], axis=1)
    kv_all = lax.all_gather(
        kv_low.reshape(micro_count, rows_own, 2 * kv_width), "ctx", axis=1, tiled=True
    )
    kv_all = kv_all.reshape(micro_count, stream, 2, KV_HEADS, HEAD)
    keys_all, values_all = kv_all[:, :, 0], kv_all[:, :, 1]
    query_low = query_low.reshape(micro_count, rows_own, KV_HEADS, groups, HEAD)
    scores = (
        jnp.einsum("mqkgd,mskd->mkgqs", query_low, keys_all, preferred_element_type=f32)
        * score_scale
    )
    scores = jnp.where(allowed[:, None, None], scores, -1e30)
    soft_probs = jax.nn.softmax(scores, axis=-1)
    probs_low = soft_probs.astype(bf16)
    mixed = jnp.einsum("mkgqs,mskd->mqkgd", probs_low, values_all, preferred_element_type=f32)
    mixed_low = mixed.reshape(rows, HEADS * HEAD).astype(bf16)
    second = x_float + jnp.dot(mixed_low, w_out, preferred_element_type=f32)
    normed_two, norm_two_pull = jax.vjp(rms_norm, second, gain_two.astype(f32))
    two_low = normed_two.astype(bf16)

    two_all = lax.all_gather(two_low, ("lo", "ctx"), axis=0, tiled=True)
    ffn_all = ffn_all.reshape(far, 3, units, D).transpose(1, 0, 2, 3).reshape(3, far * units, D)
    w_gate, w_up, w_down = ffn_all[0], ffn_all[1], ffn_all[2]
    d_hidden = jnp.einsum("td,fd->tf", cot_all, w_down, preferred_element_type=f32)
    gate_out = jnp.einsum("td,fd->tf", two_all, w_gate, preferred_element_type=f32)
    up_out = jnp.einsum("td,fd->tf", two_all, w_up, preferred_element_type=f32)
    sig = jax.nn.sigmoid(gate_out)
    silu = gate_out * sig
    hidden_low = (silu * up_out).astype(bf16)
    gate_low = (d_hidden * up_out * sig * (1.0 + gate_out * (1.0 - sig))).astype(bf16)
    up_low = (d_hidden * silu).astype(bf16)
    d_two_part = jnp.einsum("tf,fd->td", gate_low, w_gate, preferred_element_type=f32)
    d_two_part += jnp.einsum("tf,fd->td", up_low, w_up, preferred_element_type=f32)
    d_two = lax.psum_scatter(
        d_two_part.astype(bf16), ("lo", "ctx"), scatter_dimension=0, tiled=True
    ).astype(f32)
    out_part = jnp.einsum("tf,fd->td", hidden_low, w_down, preferred_element_type=f32)
    out_sum = lax.psum_scatter(
        out_part.astype(bf16), ("lo", "ctx"), scatter_dimension=0, tiled=True
    ).astype(f32)
    result = (second + out_sum).astype(bf16)
    grad_gate = jnp.einsum("tf,td->fd", gate_low, two_all, preferred_element_type=f32)
    grad_up = jnp.einsum("tf,td->fd", up_low, two_all, preferred_element_type=f32)
    grad_down = jnp.einsum("tf,td->fd", hidden_low, cot_all, preferred_element_type=f32)
    ffn_part = jnp.stack([grad_gate, grad_up, grad_down], axis=0).astype(bf16)
    ffn_grad = lax.psum_scatter(ffn_part, "hi", scatter_dimension=1, tiled=True).astype(f32)

    d_second_part, d_gain_two = norm_two_pull(d_two)
    d_second = cot_low.astype(f32) + d_second_part
    branch_low = d_second.astype(bf16)
    d_mixed = jnp.einsum("te,de->td", branch_low, w_out, preferred_element_type=f32)
    dmix_low = d_mixed.astype(bf16).reshape(micro_count, rows_own, KV_HEADS, groups, HEAD)
    d_probs = jnp.einsum("mqkgd,mskd->mkgqs", dmix_low, values_all, preferred_element_type=f32)
    row_delta = jnp.sum(soft_probs * d_probs, axis=-1, keepdims=True)
    dscore_low = (soft_probs * (d_probs - row_delta)).astype(bf16)
    dq_rot = (
        jnp.einsum("mkgqs,mskd->mqkgd", dscore_low, keys_all, preferred_element_type=f32)
        * score_scale
    )
    dk_part = (
        jnp.einsum("mkgqs,mqkgd->mskd", dscore_low, query_low, preferred_element_type=f32)
        * score_scale
    )
    dv_part = jnp.einsum("mkgqs,mqkgd->mskd", probs_low, dmix_low, preferred_element_type=f32)
    dkv_part = jnp.concatenate(
        [
            dk_part.reshape(micro_count, stream, kv_width),
            dv_part.reshape(micro_count, stream, kv_width),
        ],
        axis=2,
    )
    dkv = lax.psum_scatter(dkv_part.astype(bf16), "ctx", scatter_dimension=1, tiled=True)
    dkv = dkv.reshape(rows, 2 * kv_width)
    dq_low = (
        rotate_back(dq_rot.reshape(rows, HEADS, HEAD), cos_heads, sin_heads)
        .reshape(rows, HEADS * HEAD)
        .astype(bf16)
    )
    dk_rot = dkv[:, :kv_width].astype(f32).reshape(rows, KV_HEADS, HEAD)
    dk_low = rotate_back(dk_rot, cos_heads, sin_heads).reshape(rows, kv_width).astype(bf16)
    d_qkv = jnp.concatenate([dq_low, dk_low, dkv[:, kv_width:]], axis=1)
    d_normed = jnp.einsum("te,de->td", d_qkv, w_qkv, preferred_element_type=f32)
    d_input_part, d_gain_one = norm_pull(d_normed)
    input_grad = (d_second + d_input_part).astype(bf16)
    grad_qkv = jnp.einsum("td,te->de", normed_low, d_qkv, preferred_element_type=f32)
    grad_out = jnp.einsum("td,te->de", mixed_low, branch_low, preferred_element_type=f32)
    grad_bias = jnp.sum(d_qkv.astype(f32), axis=0)
    pieces = [
        grad_qkv[:, :D],
        grad_qkv[:, D : D + kv_width],
        grad_qkv[:, D + kv_width :],
        grad_out,
        grad_bias,
        d_gain_one,
        d_gain_two,
    ]
    flat_grad = pack_grads(pieces, total_length)
    attn_grad = lax.psum_scatter(
        flat_grad.astype(bf16).reshape(devices, -1, 128),
        ("hi", "lo", "ctx"),
        scatter_dimension=0,
        tiled=True,
    ).astype(f32)
    shape = tokens.shape
    return (result.reshape(shape), input_grad.reshape(shape), attn_grad.reshape(-1), ffn_grad)


def solution(mesh):
    grid = mesh.devices
    split = Mesh(grid.reshape(grid.shape[0] // 2, 2, grid.shape[1]), ("hi", "lo", "ctx"))
    every = ("hi", "lo", "ctx")
    return jax.shard_map(
        per_device,
        mesh=split,
        in_specs=(
            P(None, every, None),
            P(("hi", "lo"), None, None),
            P(every),
            P(None, every, None),
            P(None, every, None),
        ),
        out_specs=(
            P(None, every, None),
            P(None, every, None),
            P(every),
            P(None, every, None),
        ),
        check_vma=False,
    )
```

```python
import functools

import jax
import jax.numpy as jnp
from jax import lax
from jax.experimental import pallas as pl
from jax.experimental.pallas import tpu as pltpu
from jax.sharding import Mesh
from jax.sharding import PartitionSpec as P

D = 896
HEADS = 14
KV_HEADS = 2
HEAD = 64


EPSILON = 1e-06
THETA = 1000000.0


def rms_norm(values, gain_vec):
    return (
        values * lax.rsqrt(jnp.mean(values * values, axis=-1, keepdims=True) + EPSILON) * gain_vec
    )


def rotate(values, cosine, sine_table):
    half_width = values.shape[-1] // 2
    turned = jnp.concatenate([-values[..., half_width:], values[..., :half_width]], axis=-1)
    return values * cosine + turned * sine_table


def rotate_back(incoming, cosine, sine_table):
    scaled = incoming * sine_table
    half_width = incoming.shape[-1] // 2
    turned = jnp.concatenate([scaled[..., half_width:], -scaled[..., :half_width]], axis=-1)
    return incoming * cosine + turned


def geometry(seq_lens, slot_ids):
    seq_ends = jnp.cumsum(seq_lens)
    seq_starts = seq_ends - seq_lens
    filled = seq_ends[-1]
    numbers = jnp.arange(seq_lens.shape[0], dtype=jnp.int32)
    segment = jnp.sum((slot_ids[:, None] >= seq_ends[None, :]).astype(jnp.int32), axis=1)
    seq_begin = jnp.sum(
        jnp.where(segment[:, None] == numbers[None, :], seq_starts[None, :], 0), axis=1
    )
    inside = slot_ids < filled
    segment = jnp.where(inside, segment, seq_lens.shape[0] + slot_ids)
    position = jnp.where(inside, slot_ids - seq_begin, 0)
    return (segment, position)


def rotary_tables(position):
    half_width = HEAD // 2
    frequency = jnp.power(THETA, -(jnp.arange(half_width, dtype=jnp.float32) * 2.0 / HEAD))
    angles = position.astype(jnp.float32)[:, None] * frequency[None, :]
    cosine = jnp.concatenate([jnp.cos(angles), jnp.cos(angles)], axis=-1)
    sine_table = jnp.concatenate([jnp.sin(angles), jnp.sin(angles)], axis=-1)
    return (cosine, sine_table)


QKV = (HEADS + 2 * KV_HEADS) * HEAD
LANES = 128
W = D // LANES
MATRIX_ROWS = 2 * D * W + 2 * D * KV_HEADS * HEAD // LANES
SMALL_ROWS = 24
MESH = pl.DeviceIdType.MESH


class Place:
    def __init__(self, ctx):
        self.ctx = ctx
        self.hi = lax.axis_index("hi")
        self.lo = lax.axis_index("lo")
        self.c = lax.axis_index("ctx")
        self.sib = self.c + 1 - 2 * lax.rem(self.c, 2)
        self.rels = [(a, b) for a in range(2) for b in range(ctx // 2)]
        self.n = len(self.rels)

    def to(self, r, c=None):
        a, b = self.rels[r]
        c = self.c if c is None else c
        return lax.rem(self.lo + a, 2), lax.rem(c + 2 * b, self.ctx)

    def source(self, r, c=None):
        a, b = self.rels[r]
        c = self.c if c is None else c
        return lax.rem(self.lo + 2 - a, 2), lax.rem(c + self.ctx - 2 * b, self.ctx)

    def slot(self, pair):
        return pair[0] * self.ctx + pair[1]

    def cube(self):
        return [(self.hi,) + self.to(r) for r in range(1, self.n)] + [self.sibling()]

    def sibling(self):
        return (self.hi, self.lo, self.sib)


def greet(devices):
    barrier = pltpu.get_barrier_semaphore()
    for device in devices:
        pl.semaphore_signal(barrier, inc=1, device_id=device, device_id_type=MESH)
    pl.semaphore_wait(barrier, len(devices))


def remote(src, dst, send, recv, device):
    return pltpu.make_async_remote_copy(
        src_ref=src, dst_ref=dst, send_sem=send, recv_sem=recv,
        device_id=device, device_id_type=MESH,
    )


class CubeGather:
    def __init__(self, at, own, out, sems, aim=lambda out, slot: out.at[slot]):
        self.at, self.own, self.out, self.aim = at, own, out, aim
        self.send1, self.recv1, self.send2, self.recv2 = sems
        self.started = []

    def go(self, copy):
        copy.start()
        self.started.append(copy)

    def push(self):
        at = self.at
        mine = self.aim(self.out, at.slot((at.lo, at.c)))
        for r in range(1, at.n):
            self.go(remote(self.own, mine, self.send1.at[r], self.recv1.at[r], (at.hi,) + at.to(r)))
        self.go(remote(self.own, mine, self.send2.at[0], self.recv2.at[0], at.sibling()))

    def forward(self):
        at = self.at
        for r in range(1, at.n):
            here = self.aim(self.out, at.slot(at.source(r)))
            remote(here, here, self.send1.at[r], self.recv1.at[r], (at.hi,) + at.to(r)).wait_recv()
            self.go(remote(here, here, self.send2.at[r], self.recv2.at[r], at.sibling()))

    def finish(self):
        at = self.at
        for r in range(at.n):
            here = self.aim(self.out, at.slot(at.source(r, at.sib)))
            remote(here, here, self.send2.at[r], self.recv2.at[r], at.sibling()).wait_recv()
        for copy in self.started:
            copy.wait_send()


class CubeScatter:
    def __init__(self, at, part, bufs, sems):
        self.at, self.part = at, part
        self.buf1, self.tmp, self.buf2 = bufs
        self.send1, self.recv1, self.send2, self.recv2 = sems
        self.started = []

    def go(self, copy):
        copy.start()
        self.started.append(copy)

    def push(self):
        at = self.at
        for r in list(range(1, at.n)) + [0]:
            there = at.slot(at.to(r, at.sib))
            self.go(remote(self.part.at[there], self.buf1.at[r], self.send1.at[r], self.recv1.at[r], at.sibling()))

    def arrived(self, r):
        at = self.at
        remote(self.buf1.at[r], self.buf1.at[r], self.send1.at[r], self.recv1.at[r], at.sibling()).wait_recv()
        mine = self.part[at.slot(at.to(r))].astype(jnp.float32)
        return mine + self.buf1[r].astype(jnp.float32)

    def forward(self):
        at = self.at
        for r in range(1, at.n):
            self.tmp[r] = self.arrived(r).astype(jnp.bfloat16)
            self.go(remote(self.tmp.at[r], self.buf2.at[r], self.send2.at[r], self.recv2.at[r], (at.hi,) + at.to(r)))

    def finish(self):
        at = self.at
        total = self.arrived(0)
        for r in range(1, at.n):
            remote(self.buf2.at[r], self.buf2.at[r], self.send2.at[r], self.recv2.at[r], (at.hi,) + at.to(r)).wait_recv()
            total = total + self.buf2[r].astype(jnp.float32)
        return total

    def drain(self):
        for copy in self.started:
            copy.wait_send()


def params_kernel(far, ctx, shard, pad, *refs):
    attn_ref, cot_ref, qkv_ref, wout_ref, small_ref, cots_ref, held, flat = refs[:8]
    send_z, recv_z = refs[8:10]
    piece_sems, cot_sems = refs[10:14], refs[14:18]
    at = Place(ctx)
    beyond = [(lax.rem(at.hi + h, far), at.lo, at.c) for h in range(1, far)]
    greet(at.cube() + beyond)
    mine = at.slot((at.lo, at.c))
    for h in range(1, far):
        remote(attn_ref, held.at[mine, at.hi], send_z.at[h], recv_z.at[h], beyond[h - 1]).start()
    gathers = []
    for h in range(far):
        origin = lax.rem(at.hi + far - h, far)
        own = attn_ref if h == 0 else held.at[mine, origin]
        if h:
            remote(own, own, send_z.at[h], recv_z.at[h], beyond[h - 1]).wait_recv()
        gather = CubeGather(
            at, own, held, [s.at[h] for s in piece_sems],
            lambda out, slot, origin=origin: out.at[slot, origin],
        )
        gather.push()
        gathers.append(gather)
    held[mine, at.hi] = attn_ref[...]
    cots = CubeGather(at, cot_ref, cots_ref, cot_sems)
    cots.push()
    cots_ref[mine] = cot_ref[...]
    for gather in gathers:
        gather.forward()
    cots.forward()
    for gather in gathers:
        gather.finish()
    for g in range(0, far * 2 * ctx):
        block = held[g % (2 * ctx), g // (2 * ctx)].astype(jnp.float32)
        flat[pl.ds(g * shard, pad), :] = block
    for j in range(W):
        cols = pl.ds(j * LANES, LANES)
        qkv_ref[:, cols] = flat[pl.ds(j, D, stride=W), :].astype(jnp.bfloat16)
        wout_ref[:, cols] = flat[pl.ds(D * W + 2 * D + j, D, stride=W), :].astype(jnp.bfloat16)
    for j in range(2):
        cols = pl.ds(D + j * LANES, LANES)
        qkv_ref[:, cols] = flat[pl.ds(D * W + j * D, D), :].astype(jnp.bfloat16)
    small_ref[...] = flat[pl.ds(MATRIX_ROWS, SMALL_ROWS), :]
    cots.finish()
    for h in range(1, far):
        remote(attn_ref, held.at[mine, at.hi], send_z.at[h], recv_z.at[h], beyond[h - 1]).wait_send()


def rows_kernel(ctx, own_ref, out_ref, *sems):
    at = Place(ctx)
    greet(at.cube())
    gather = CubeGather(at, own_ref, out_ref, sems)
    gather.push()
    out_ref[at.slot((at.lo, at.c))] = own_ref[...]
    gather.forward()
    gather.finish()


def sum_kernel(ctx, part_ref, out_ref, buf1, tmp, buf2, *sems):
    at = Place(ctx)
    greet(at.cube())
    scatter = CubeScatter(at, part_ref, (buf1, tmp, buf2), sems)
    scatter.push()
    scatter.forward()
    out_ref[...] = scatter.finish()
    scatter.drain()


def stream_sum_kernel(ctx, part_ref, out_ref, buf, send, recv):
    hi, lo, c = lax.axis_index("hi"), lax.axis_index("lo"), lax.axis_index("ctx")
    others = [lax.rem(c + d, ctx) for d in range(1, ctx)]
    greet([(hi, lo, other) for other in others])
    copies = []
    for d, other in enumerate(others):
        copy = remote(part_ref.at[other], buf.at[d], send.at[d], recv.at[d], (hi, lo, other))
        copy.start()
        copies.append(copy)
    total = part_ref[c].astype(jnp.float32)
    for d, copy in enumerate(copies):
        copy.wait()
        total = total + buf[d].astype(jnp.float32)
    out_ref[...] = total


def grads_kernel(far, ctx, shard, pad, *refs):
    qkv_ref, gout_ref, small_ref, part_ref, attn_ref, sum_ref = refs[:6]
    flat, held, col, low, buf3 = refs[6:11]
    attn_bufs, sum_bufs = refs[11:14], refs[14:17]
    send_z, recv_z = refs[17:19]
    attn_sems, sum_sems = refs[19:23], refs[23:27]
    at = Place(ctx)
    beyond = [(lax.rem(at.hi + h, far), at.lo, at.c) for h in range(1, far)]
    greet(at.cube() + beyond)
    sums = CubeScatter(at, part_ref, sum_bufs, sum_sems)
    sums.push()
    for j in range(W):
        cols = pl.ds(j * LANES, LANES)
        flat[pl.ds(j, D, stride=W), :] = qkv_ref[:, cols]
        flat[pl.ds(D * W + 2 * D + j, D, stride=W), :] = gout_ref[:, cols]
    for j in range(2):
        flat[pl.ds(D * W + j * D, D), :] = qkv_ref[:, pl.ds(D + j * LANES, LANES)]
    flat[pl.ds(MATRIX_ROWS, SMALL_ROWS), :] = small_ref[...]
    tail = MATRIX_ROWS + SMALL_ROWS
    flat[pl.ds(tail, flat.shape[0] - tail), :] = jnp.zeros((flat.shape[0] - tail, LANES), jnp.float32)
    for g in range(far * 2 * ctx):
        block = flat[pl.ds(g * shard, pad), :]
        held[g % (2 * ctx), g // (2 * ctx)] = block.astype(jnp.bfloat16)
    grads = CubeScatter(at, held, attn_bufs, attn_sems)
    grads.push()
    grads.forward()
    sums.forward()
    col[...] = grads.finish()
    low[...] = col[...].astype(jnp.bfloat16)
    crossing = []
    for h in range(1, far):
        copy = remote(low.at[beyond[h - 1][0]], buf3.at[h], send_z.at[h], recv_z.at[h], beyond[h - 1])
        copy.start()
        crossing.append(copy)
    sum_ref[...] = sums.finish()
    total = col[at.hi]
    for h in range(1, far):
        crossing[h - 1].wait()
        total = total + buf3[h].astype(jnp.float32)
    attn_ref[...] = total
    grads.drain()
    sums.drain()


def call(kernel, outs, scratch, number, *args):
    vmem = pl.BlockSpec(memory_space=pltpu.VMEM)
    return pl.pallas_call(
        kernel,
        out_shape=[jax.ShapeDtypeStruct(shape, kind) for shape, kind in outs],
        in_specs=[vmem] * len(args),
        out_specs=[vmem] * len(outs),
        scratch_shapes=scratch,
        compiler_params=pltpu.CompilerParams(
            collective_id=number, has_side_effects=True, vmem_limit_bytes=48 * 2**20
        ),
    )(*args)


def dma(*shape):
    return pltpu.SemaphoreType.DMA(shape)


def padded(shard):
    return -(-shard // 16) * 16


def gather_params(attn_rows, cot_low, far, ctx):
    shard = attn_rows.shape[0]
    pad = padded(shard)
    cube, n = 2 * ctx, ctx
    total = shard * far * cube + pad - shard
    attn_rows = jnp.pad(attn_rows, ((0, pad - shard), (0, 0)))
    bf16 = jnp.bfloat16
    outs = [
        ((D, QKV), bf16),
        ((D, D), bf16),
        ((SMALL_ROWS, LANES), jnp.float32),
        ((cube,) + cot_low.shape, bf16),
    ]
    scratch = [
        pltpu.VMEM((cube, far, pad, LANES), bf16),
        pltpu.VMEM((total, LANES), jnp.float32),
        dma(far),
        dma(far),
    ]
    scratch += [dma(far, n)] * 4 + [dma(n)] * 4
    kernel = functools.partial(params_kernel, far, ctx, shard, pad)
    return call(kernel, outs, scratch, 0, attn_rows, cot_low)


def gather_rows(rows_low, ctx):
    outs = [((2 * ctx,) + rows_low.shape, jnp.bfloat16)]
    return call(functools.partial(rows_kernel, ctx), outs, [dma(ctx)] * 4, 1, rows_low)[0]


def sum_rows(part, ctx):
    block = part.shape[1:]
    scratch = [pltpu.VMEM((ctx,) + block, jnp.bfloat16)] * 3 + [dma(ctx)] * 4
    return call(functools.partial(sum_kernel, ctx), [(block, jnp.float32)], scratch, 2, part)[0]


def stream_sum(part, ctx):
    block = part.shape[1:]
    scratch = [pltpu.VMEM((ctx - 1,) + block, jnp.bfloat16), dma(ctx - 1), dma(ctx - 1)]
    return call(functools.partial(stream_sum_kernel, ctx), [(block, jnp.float32)], scratch, 3, part)[0]


def scatter_grads(grad_qkv, grad_out, small, part, shard, far, ctx):
    pad = padded(shard)
    cube, n = 2 * ctx, ctx
    total = shard * far * cube + pad - shard
    block = part.shape[1:]
    bf16 = jnp.bfloat16
    column = (far, pad, LANES)
    scratch = [
        pltpu.VMEM((total, LANES), jnp.float32),
        pltpu.VMEM((cube,) + column, bf16),
        pltpu.VMEM(column, jnp.float32),
        pltpu.VMEM(column, bf16),
        pltpu.VMEM(column, bf16),
    ]
    scratch += [pltpu.VMEM((n,) + column, bf16)] * 3 + [pltpu.VMEM((n,) + block, bf16)] * 3
    scratch += [dma(far)] * 2 + [dma(n)] * 8
    kernel = functools.partial(grads_kernel, far, ctx, shard, pad)
    outs = [((pad, LANES), jnp.float32), (block, jnp.float32)]
    attn, out_sum = call(kernel, outs, scratch, 4, grad_qkv, grad_out, small, part)
    return attn[:shard], out_sum


def per_device(tokens, seq_lengths, attn_params, ffn_weight, out_grad):
    micro_count, rows_own = tokens.shape[0], tokens.shape[1]
    stream = rows_own * lax.axis_size("ctx")
    rows = micro_count * rows_own
    groups = HEADS // KV_HEADS
    kv_width = KV_HEADS * HEAD
    score_scale = HEAD ** (-0.5)
    units = ffn_weight.shape[1]
    far = lax.axis_size("hi")
    ctx = lax.axis_size("ctx")
    cube = 2 * ctx
    f32, bf16 = jnp.float32, jnp.bfloat16

    cot_low = out_grad.reshape(rows, D)
    ffn_all = lax.all_gather(ffn_weight.reshape(3 * units, D), "hi", axis=0, tiled=False)
    attn_rows = attn_params.reshape(-1, LANES)
    w_qkv, w_out, small, cot_all = gather_params(attn_rows, cot_low, far, ctx)
    cot_all = cot_all.reshape(-1, D)
    small = small.reshape(-1)
    b_qkv, gain_one, gain_two = small[:QKV], small[QKV : QKV + D], small[QKV + D : QKV + 2 * D]

    slot_ids = jnp.arange(stream, dtype=jnp.int32)
    first_slot = lax.axis_index("ctx") * rows_own
    own_slots = first_slot + jnp.arange(rows_own, dtype=jnp.int32)
    segment, position = jax.vmap(geometry, in_axes=(0, None))(seq_lengths[0], slot_ids)
    own_segment = lax.dynamic_slice_in_dim(segment, first_slot, rows_own, axis=1)
    own_position = lax.dynamic_slice_in_dim(position, first_slot, rows_own, axis=1)
    cosine, sine_table = rotary_tables(own_position.reshape(-1))
    cos_heads, sin_heads = cosine[:, None, :], sine_table[:, None, :]
    allowed = (own_segment[:, :, None] == segment[:, None, :]) & (
        slot_ids[None, None, :] <= own_slots[None, :, None]
    )

    x_float = tokens.reshape(rows, D).astype(f32)
    normed, norm_pull = jax.vjp(rms_norm, x_float, gain_one)
    normed_low = normed.astype(bf16)
    qkv = jnp.dot(normed_low, w_qkv, preferred_element_type=f32) + b_qkv
    query_pre, key_pre, value_pre = jnp.split(qkv, [D, D + kv_width], axis=1)
    query_low = rotate(query_pre.reshape(rows, HEADS, HEAD), cos_heads, sin_heads).astype(bf16)
    key_low = rotate(key_pre.reshape(rows, KV_HEADS, HEAD), cos_heads, sin_heads).astype(bf16)
    kv_low = jnp.concatenate([key_low.reshape(rows, kv_width), value_pre.astype(bf16)], axis=1)
    kv_all = lax.all_gather(
        kv_low.reshape(micro_count, rows_own, 2 * kv_width), "ctx", axis=1, tiled=True
    )
    kv_all = kv_all.reshape(micro_count, stream, 2, KV_HEADS, HEAD)
    keys_all, values_all = kv_all[:, :, 0], kv_all[:, :, 1]
    query_low = query_low.reshape(micro_count, rows_own, KV_HEADS, groups, HEAD)
    scores = (
        jnp.einsum("mqkgd,mskd->mkgqs", query_low, keys_all, preferred_element_type=f32)
        * score_scale
    )
    scores = jnp.where(allowed[:, None, None], scores, -1e30)
    soft_probs = jax.nn.softmax(scores, axis=-1)
    probs_low = soft_probs.astype(bf16)
    mixed = jnp.einsum("mkgqs,mskd->mqkgd", probs_low, values_all, preferred_element_type=f32)
    mixed_low = mixed.reshape(rows, HEADS * HEAD).astype(bf16)
    second = x_float + jnp.dot(mixed_low, w_out, preferred_element_type=f32)
    normed_two, norm_two_pull = jax.vjp(rms_norm, second, gain_two)
    two_low = normed_two.astype(bf16)

    two_all = gather_rows(two_low, ctx).reshape(-1, D)
    ffn_all = ffn_all.reshape(far, 3, units, D).transpose(1, 0, 2, 3).reshape(3, far * units, D)
    w_gate, w_up, w_down = ffn_all[0], ffn_all[1], ffn_all[2]
    d_hidden = jnp.einsum("td,fd->tf", cot_all, w_down, preferred_element_type=f32)
    gate_out = jnp.einsum("td,fd->tf", two_all, w_gate, preferred_element_type=f32)
    up_out = jnp.einsum("td,fd->tf", two_all, w_up, preferred_element_type=f32)
    sig = jax.nn.sigmoid(gate_out)
    silu = gate_out * sig
    hidden_low = (silu * up_out).astype(bf16)
    gate_low = (d_hidden * up_out * sig * (1.0 + gate_out * (1.0 - sig))).astype(bf16)
    up_low = (d_hidden * silu).astype(bf16)
    d_two_part = jnp.einsum("tf,fd->td", gate_low, w_gate, preferred_element_type=f32)
    d_two_part += jnp.einsum("tf,fd->td", up_low, w_up, preferred_element_type=f32)
    d_two = sum_rows(d_two_part.astype(bf16).reshape(cube, rows, D), ctx)
    out_part = jnp.einsum("tf,fd->td", hidden_low, w_down, preferred_element_type=f32)
    grad_gate = jnp.einsum("tf,td->fd", gate_low, two_all, preferred_element_type=f32)
    grad_up = jnp.einsum("tf,td->fd", up_low, two_all, preferred_element_type=f32)
    grad_down = jnp.einsum("tf,td->fd", hidden_low, cot_all, preferred_element_type=f32)
    ffn_part = jnp.stack([grad_gate.astype(bf16), grad_up.astype(bf16), grad_down.astype(bf16)])
    ffn_part = ffn_part.reshape(3, far, units, D).transpose(1, 0, 2, 3).reshape(far, 3 * units, D)
    ffn_grad = lax.psum_scatter(ffn_part, "hi", scatter_dimension=0, tiled=False)
    ffn_grad = ffn_grad.astype(f32).reshape(3, units, D)

    d_second_part, d_gain_two = norm_two_pull(d_two)
    d_second = cot_low.astype(f32) + d_second_part
    branch_low = d_second.astype(bf16)
    d_mixed = jnp.einsum("te,de->td", branch_low, w_out, preferred_element_type=f32)
    dmix_low = d_mixed.astype(bf16).reshape(micro_count, rows_own, KV_HEADS, groups, HEAD)
    d_probs = jnp.einsum("mqkgd,mskd->mkgqs", dmix_low, values_all, preferred_element_type=f32)
    row_delta = jnp.sum(soft_probs * d_probs, axis=-1, keepdims=True)
    dscore_low = (soft_probs * (d_probs - row_delta)).astype(bf16)
    dq_rot = (
        jnp.einsum("mkgqs,mskd->mqkgd", dscore_low, keys_all, preferred_element_type=f32)
        * score_scale
    )
    dk_part = (
        jnp.einsum("mkgqs,mqkgd->mskd", dscore_low, query_low, preferred_element_type=f32)
        * score_scale
    )
    dv_part = jnp.einsum("mkgqs,mqkgd->mskd", probs_low, dmix_low, preferred_element_type=f32)
    dkv_part = jnp.concatenate(
        [
            dk_part.reshape(micro_count, stream, kv_width),
            dv_part.reshape(micro_count, stream, kv_width),
        ],
        axis=2,
    )
    dkv_part = dkv_part.astype(bf16).reshape(micro_count, ctx, rows_own, 2 * kv_width)
    dkv = stream_sum(dkv_part.transpose(1, 0, 2, 3).reshape(ctx, rows, 2 * kv_width), ctx)
    dq_low = (
        rotate_back(dq_rot.reshape(rows, HEADS, HEAD), cos_heads, sin_heads)
        .reshape(rows, HEADS * HEAD)
        .astype(bf16)
    )
    dk_rot = dkv[:, :kv_width].reshape(rows, KV_HEADS, HEAD)
    dk_low = rotate_back(dk_rot, cos_heads, sin_heads).reshape(rows, kv_width).astype(bf16)
    d_qkv = jnp.concatenate([dq_low, dk_low, dkv[:, kv_width:].astype(bf16)], axis=1)
    d_normed = jnp.einsum("te,de->td", d_qkv, w_qkv, preferred_element_type=f32)
    d_input_part, d_gain_one = norm_pull(d_normed)
    input_grad = (d_second + d_input_part).astype(bf16)
    grad_qkv = jnp.einsum("td,te->de", normed_low, d_qkv, preferred_element_type=f32)
    grad_out = jnp.einsum("td,te->de", mixed_low, branch_low, preferred_element_type=f32)
    grad_bias = jnp.sum(d_qkv.astype(f32), axis=0)
    zeros = jnp.zeros((SMALL_ROWS * LANES - QKV - 2 * D,), f32)
    small_grad = jnp.concatenate([grad_bias, d_gain_one, d_gain_two, zeros])
    attn_grad, out_sum = scatter_grads(
        grad_qkv,
        grad_out,
        small_grad.reshape(SMALL_ROWS, LANES),
        out_part.astype(bf16).reshape(cube, rows, D),
        attn_rows.shape[0],
        far,
        ctx,
    )
    result = (second + out_sum).astype(bf16)
    shape = tokens.shape
    return (result.reshape(shape), input_grad.reshape(shape), attn_grad.reshape(-1), ffn_grad)


def solution(mesh):
    grid = mesh.devices
    split = Mesh(grid.reshape(grid.shape[0] // 2, 2, grid.shape[1]), ("hi", "lo", "ctx"))
    every = ("hi", "lo", "ctx")
    return jax.shard_map(
        per_device,
        mesh=split,
        in_specs=(
            P(None, every, None),
            P(("hi", "lo"), None, None),
            P(every),
            P(None, every, None),
            P(None, every, None),
        ),
        out_specs=(
            P(None, every, None),
            P(None, every, None),
            P(every),
            P(None, every, None),
        ),
        check_vma=False,
    )
```

```python
import functools

import jax
import jax.numpy as jnp
from jax import lax
from jax.experimental import pallas as pl
from jax.experimental.pallas import tpu as pltpu
from jax.sharding import Mesh
from jax.sharding import PartitionSpec as P

D = 896
HEADS = 14
KV_HEADS = 2
HEAD = 64


EPSILON = 1e-06
THETA = 1000000.0


def rms_norm(values, gain_vec):
    return (
        values * lax.rsqrt(jnp.mean(values * values, axis=-1, keepdims=True) + EPSILON) * gain_vec
    )


def rotate(values, cosine, sine_table):
    half_width = values.shape[-1] // 2
    turned = jnp.concatenate([-values[..., half_width:], values[..., :half_width]], axis=-1)
    return values * cosine + turned * sine_table


def rotate_back(incoming, cosine, sine_table):
    scaled = incoming * sine_table
    half_width = incoming.shape[-1] // 2
    turned = jnp.concatenate([scaled[..., half_width:], -scaled[..., :half_width]], axis=-1)
    return incoming * cosine + turned


def geometry(seq_lens, slot_ids):
    seq_ends = jnp.cumsum(seq_lens)
    seq_starts = seq_ends - seq_lens
    filled = seq_ends[-1]
    numbers = jnp.arange(seq_lens.shape[0], dtype=jnp.int32)
    segment = jnp.sum((slot_ids[:, None] >= seq_ends[None, :]).astype(jnp.int32), axis=1)
    seq_begin = jnp.sum(
        jnp.where(segment[:, None] == numbers[None, :], seq_starts[None, :], 0), axis=1
    )
    inside = slot_ids < filled
    segment = jnp.where(inside, segment, seq_lens.shape[0] + slot_ids)
    position = jnp.where(inside, slot_ids - seq_begin, 0)
    return (segment, position)


def rotary_tables(position):
    half_width = HEAD // 2
    frequency = jnp.power(THETA, -(jnp.arange(half_width, dtype=jnp.float32) * 2.0 / HEAD))
    angles = position.astype(jnp.float32)[:, None] * frequency[None, :]
    cosine = jnp.concatenate([jnp.cos(angles), jnp.cos(angles)], axis=-1)
    sine_table = jnp.concatenate([jnp.sin(angles), jnp.sin(angles)], axis=-1)
    return (cosine, sine_table)


QKV = (HEADS + 2 * KV_HEADS) * HEAD
LANES = 128
W = D // LANES
MATRIX_ROWS = 2 * D * W + 2 * D * KV_HEADS * HEAD // LANES
SMALL_ROWS = 24
MESH = pl.DeviceIdType.MESH
NEAR = [(0, 0), (0, 1), (1, 0), (1, 1)]
N = len(NEAR)


class Place:
    def __init__(self, ctx):
        self.ctx = ctx
        self.hi = lax.axis_index("hi")
        self.lo = lax.axis_index("lo")
        self.c = lax.axis_index("ctx")
        self.sib = self.c + 1 - 2 * lax.rem(self.c, 2)

    def of(self, r, c=None):
        c = self.c if c is None else c
        a, b = NEAR[r]
        return lax.rem(self.lo + a, 2), lax.rem(c + 2 * b, self.ctx)

    def slot(self, r, c=None):
        lo, c = self.of(r, c)
        return lo * self.ctx + c

    def device(self, r):
        return (self.hi,) + self.of(r)

    def sibling(self):
        return (self.hi, self.lo, self.sib)

    def cube(self):
        return [self.device(1), self.device(2), self.sibling()]


def greet(devices):
    barrier = pltpu.get_barrier_semaphore()
    for device in devices:
        pl.semaphore_signal(barrier, inc=1, device_id=device, device_id_type=MESH)
    pl.semaphore_wait(barrier, len(devices))


def remote(src, dst, send, recv, device):
    return pltpu.make_async_remote_copy(
        src_ref=src, dst_ref=dst, send_sem=send, recv_sem=recv,
        device_id=device, device_id_type=MESH,
    )


class Unit:
    def __init__(self, at, turn, sems):
        self.at = at
        self.first, self.second = (1, 2) if turn % 2 == 0 else (2, 1)
        self.send1, self.recv1, self.send2, self.recv2 = sems
        self.started = []

    def go(self, *parts):
        copy = remote(*parts)
        copy.start()
        self.started.append(copy)

    def drain(self):
        for copy in self.started:
            copy.wait_send()


class CubeGather(Unit):
    def __init__(self, at, turn, own, aim, sems):
        super().__init__(at, turn, sems)
        self.own, self.aim = own, aim

    def push(self):
        at = self.at
        mine = self.aim(at.slot(0))
        for r in (self.first, self.second):
            self.go(self.own, mine, self.send1.at[r], self.recv1.at[r], at.device(r))
        self.go(self.own, mine, self.send2.at[0], self.recv2.at[0], at.sibling())

    def arrive(self, r, by):
        at = self.at
        here = self.aim(at.slot(r))
        remote(here, here, self.send1.at[r], self.recv1.at[r], at.device(by)).wait_recv()
        if r == self.first:
            self.go(here, here, self.send1.at[3], self.recv1.at[3], at.device(self.second))
        self.go(here, here, self.send2.at[r], self.recv2.at[r], at.sibling())

    def forward(self):
        self.arrive(self.first, self.first)
        self.arrive(self.second, self.second)

    def corner(self):
        self.arrive(3, self.second)

    def finish(self):
        at = self.at
        for r in range(N):
            here = self.aim(at.slot(r, at.sib))
            remote(here, here, self.send2.at[r], self.recv2.at[r], at.sibling()).wait_recv()
        self.drain()


class CubeScatter(Unit):
    def __init__(self, at, turn, part, bufs, sems):
        super().__init__(at, turn, sems)
        self.part = part
        self.buf1, self.tmp, self.buf2 = bufs

    def push(self):
        at = self.at
        for r in (3, self.first, self.second, 0):
            there = self.part(at.slot(r, at.sib))
            self.go(there, self.buf1.at[r], self.send1.at[r], self.recv1.at[r], at.sibling())

    def arrived(self, r):
        at, buf = self.at, self.buf1.at[r]
        remote(buf, buf, self.send1.at[r], self.recv1.at[r], at.sibling()).wait_recv()
        return self.part(at.slot(r))[...].astype(jnp.float32) + buf[...].astype(jnp.float32)

    def landed(self, r, by):
        buf = self.buf2.at[r]
        remote(buf, buf, self.send2.at[r], self.recv2.at[r], self.at.device(by)).wait_recv()
        return buf[...].astype(jnp.float32)

    def send(self, r, value, to):
        self.tmp[r] = value.astype(jnp.bfloat16)
        self.go(self.tmp.at[r], self.buf2.at[r], self.send2.at[r], self.recv2.at[r], self.at.device(to))

    def forward(self):
        self.send(3, self.arrived(3), self.first)
        self.send(self.first, self.arrived(self.first), self.first)

    def corner(self):
        value = self.arrived(self.second)
        self.send(self.second, value + self.landed(3, self.first), self.second)

    def finish(self):
        total = self.arrived(0)
        for r in (self.first, self.second):
            total = total + self.landed(r, r)
        return total


def row_units(rows):
    half = rows // 2
    return [pl.ds(u * half, half) for u in range(2)]


def row_gathers(at, own, out, sems):
    return [
        CubeGather(at, u, own.at[span], lambda slot, span=span: out.at[slot, span], [s.at[u] for s in sems])
        for u, span in enumerate(row_units(own.shape[0]))
    ]


def row_scatters(at, part, bufs, sems):
    return [
        CubeScatter(
            at, u, lambda slot, span=span: part.at[slot, span],
            [b.at[u] for b in bufs], [s.at[u] for s in sems],
        )
        for u, span in enumerate(row_units(part.shape[1]))
    ]


def params_kernel(far, ctx, shard, pad, *refs):
    attn_ref, cot_ref, qkv_ref, wout_ref, small_ref, cots_ref, held, flat = refs[:8]
    send_z, recv_z = refs[8:10]
    piece_sems, cot_sems = refs[10:14], refs[14:18]
    at = Place(ctx)
    beyond = [(lax.rem(at.hi + h, far), at.lo, at.c) for h in range(1, far)]
    greet(at.cube() + beyond)
    mine = at.slot(0)
    for h in range(1, far):
        remote(attn_ref, held.at[mine, at.hi], send_z.at[h], recv_z.at[h], beyond[h - 1]).start()
    cots = row_gathers(at, cot_ref, cots_ref, cot_sems)
    gathers = []
    for h in range(far):
        origin = lax.rem(at.hi + far - h, far)
        own = attn_ref if h == 0 else held.at[mine, origin]
        if h:
            remote(own, own, send_z.at[h], recv_z.at[h], beyond[h - 1]).wait_recv()
        gather = CubeGather(
            at, h, own, lambda slot, origin=origin: held.at[slot, origin],
            [s.at[h] for s in piece_sems],
        )
        gather.push()
        gathers.append(gather)
        if h == 0:
            held[mine, at.hi] = attn_ref[...]
            for cot in cots:
                cot.push()
            cots_ref[mine] = cot_ref[...]
    for gather in gathers:
        gather.forward()
    for gather in gathers:
        gather.corner()
    for cot in cots:
        cot.forward()
    for cot in cots:
        cot.corner()
    for gather in gathers:
        gather.finish()
    for g in range(0, far * 2 * ctx):
        block = held[g % (2 * ctx), g // (2 * ctx)].astype(jnp.float32)
        flat[pl.ds(g * shard, pad), :] = block
    for j in range(W):
        cols = pl.ds(j * LANES, LANES)
        qkv_ref[:, cols] = flat[pl.ds(j, D, stride=W), :].astype(jnp.bfloat16)
        wout_ref[:, cols] = flat[pl.ds(D * W + 2 * D + j, D, stride=W), :].astype(jnp.bfloat16)
    for j in range(2):
        cols = pl.ds(D + j * LANES, LANES)
        qkv_ref[:, cols] = flat[pl.ds(D * W + j * D, D), :].astype(jnp.bfloat16)
    small_ref[...] = flat[pl.ds(MATRIX_ROWS, SMALL_ROWS), :]
    for cot in cots:
        cot.finish()
    for h in range(1, far):
        remote(attn_ref, held.at[mine, at.hi], send_z.at[h], recv_z.at[h], beyond[h - 1]).wait_send()


def rows_kernel(ctx, own_ref, out_ref, *sems):
    at = Place(ctx)
    greet(at.cube())
    gathers = row_gathers(at, own_ref, out_ref, sems)
    for gather in gathers:
        gather.push()
    out_ref[at.slot(0)] = own_ref[...]
    for gather in gathers:
        gather.forward()
    for gather in gathers:
        gather.corner()
    for gather in gathers:
        gather.finish()


def sum_kernel(ctx, part_ref, out_ref, buf1, tmp, buf2, *sems):
    at = Place(ctx)
    greet(at.cube())
    scatters = row_scatters(at, part_ref, (buf1, tmp, buf2), sems)
    for scatter in scatters:
        scatter.push()
    for scatter in scatters:
        scatter.forward()
    for scatter in scatters:
        scatter.corner()
    for scatter, span in zip(scatters, row_units(out_ref.shape[0])):
        out_ref[span, :] = scatter.finish()
        scatter.drain()


def stream_gather_kernel(ctx, own_ref, out_ref, send, recv):
    hi, lo, c = lax.axis_index("hi"), lax.axis_index("lo"), lax.axis_index("ctx")
    others = [lax.rem(c + d, ctx) for d in range(1, ctx)]
    greet([(hi, lo, other) for other in others])
    for d, other in enumerate(others):
        remote(own_ref, out_ref.at[c], send.at[d], recv.at[d], (hi, lo, other)).start()
    out_ref[c] = own_ref[...]
    for d, other in enumerate(others):
        here = out_ref.at[lax.rem(c + ctx - d - 1, ctx)]
        remote(own_ref, here, send.at[d], recv.at[d], (hi, lo, other)).wait()


def stream_sum_kernel(ctx, part_ref, out_ref, buf, send, recv):
    hi, lo, c = lax.axis_index("hi"), lax.axis_index("lo"), lax.axis_index("ctx")
    others = [lax.rem(c + d, ctx) for d in range(1, ctx)]
    greet([(hi, lo, other) for other in others])
    copies = []
    for d, other in enumerate(others):
        copy = remote(part_ref.at[other], buf.at[d], send.at[d], recv.at[d], (hi, lo, other))
        copy.start()
        copies.append(copy)
    total = part_ref[c].astype(jnp.float32)
    for d, copy in enumerate(copies):
        copy.wait()
        total = total + buf[d].astype(jnp.float32)
    out_ref[...] = total


def grads_kernel(far, ctx, shard, pad, *refs):
    qkv_ref, gout_ref, small_ref, part_ref, attn_ref, sum_ref = refs[:6]
    flat, held, low, buf3 = refs[6:10]
    attn_bufs, sum_bufs = refs[10:13], refs[13:16]
    send_z, recv_z = refs[16:18]
    attn_sems, sum_sems = refs[18:22], refs[22:26]
    at = Place(ctx)
    beyond = [(lax.rem(at.hi + h, far), at.lo, at.c) for h in range(1, far)]
    greet(at.cube() + beyond)
    sums = row_scatters(at, part_ref, sum_bufs, sum_sems)
    for unit in sums:
        unit.push()
    for j in range(W):
        cols = pl.ds(j * LANES, LANES)
        flat[pl.ds(j, D, stride=W), :] = qkv_ref[:, cols]
        flat[pl.ds(D * W + 2 * D + j, D, stride=W), :] = gout_ref[:, cols]
    for j in range(2):
        flat[pl.ds(D * W + j * D, D), :] = qkv_ref[:, pl.ds(D + j * LANES, LANES)]
    flat[pl.ds(MATRIX_ROWS, SMALL_ROWS), :] = small_ref[...]
    tail = MATRIX_ROWS + SMALL_ROWS
    flat[pl.ds(tail, flat.shape[0] - tail), :] = jnp.zeros((flat.shape[0] - tail, LANES), jnp.float32)
    for g in range(far * 2 * ctx):
        block = flat[pl.ds(g * shard, pad), :]
        held[g % (2 * ctx), g // (2 * ctx)] = block.astype(jnp.bfloat16)
    grads = []
    for h in list(range(1, far)) + [0]:
        origin = lax.rem(at.hi + h, far)
        unit = CubeScatter(
            at, h, lambda slot, origin=origin: held.at[slot, origin],
            [b.at[h] for b in attn_bufs], [s.at[h] for s in attn_sems],
        )
        unit.push()
        grads.append(unit)
    for unit in grads:
        unit.forward()
    for unit in grads:
        unit.corner()
    for unit in sums:
        unit.forward()
    crossing = []
    for h in range(1, far):
        low[h] = grads[h - 1].finish().astype(jnp.bfloat16)
        copy = remote(low.at[h], buf3.at[h], send_z.at[h], recv_z.at[h], beyond[h - 1])
        copy.start()
        crossing.append(copy)
    total = grads[far - 1].finish()
    for unit in sums:
        unit.corner()
    for unit, span in zip(sums, row_units(sum_ref.shape[0])):
        sum_ref[span, :] = unit.finish()
    for h in range(1, far):
        crossing[h - 1].wait()
        total = total + buf3[h].astype(jnp.float32)
    attn_ref[...] = total
    for unit in grads + sums:
        unit.drain()


def call(kernel, outs, scratch, number, *args):
    vmem = pl.BlockSpec(memory_space=pltpu.VMEM)
    return pl.pallas_call(
        kernel,
        out_shape=[jax.ShapeDtypeStruct(shape, kind) for shape, kind in outs],
        in_specs=[vmem] * len(args),
        out_specs=[vmem] * len(outs),
        scratch_shapes=scratch,
        compiler_params=pltpu.CompilerParams(
            collective_id=number, has_side_effects=True, vmem_limit_bytes=48 * 2**20
        ),
    )(*args)


def dma(*shape):
    return pltpu.SemaphoreType.DMA(shape)


def padded(shard):
    return -(-shard // 16) * 16


def gather_params(attn_rows, cot_low, far, ctx):
    shard = attn_rows.shape[0]
    pad = padded(shard)
    cube = 2 * ctx
    total = shard * far * cube + pad - shard
    attn_rows = jnp.pad(attn_rows, ((0, pad - shard), (0, 0)))
    bf16 = jnp.bfloat16
    outs = [
        ((D, QKV), bf16),
        ((D, D), bf16),
        ((SMALL_ROWS, LANES), jnp.float32),
        ((cube,) + cot_low.shape, bf16),
    ]
    scratch = [
        pltpu.VMEM((cube, far, pad, LANES), bf16),
        pltpu.VMEM((total, LANES), jnp.float32),
        dma(far),
        dma(far),
    ]
    scratch += [dma(far, N)] * 4 + [dma(2, N)] * 4
    kernel = functools.partial(params_kernel, far, ctx, shard, pad)
    return call(kernel, outs, scratch, 0, attn_rows, cot_low)


def gather_rows(rows_low, ctx):
    outs = [((2 * ctx,) + rows_low.shape, jnp.bfloat16)]
    return call(functools.partial(rows_kernel, ctx), outs, [dma(2, N)] * 4, 1, rows_low)[0]


def halves(block):
    return pltpu.VMEM((2, N, block[0] // 2) + block[1:], jnp.bfloat16)


def sum_rows(part, ctx):
    block = part.shape[1:]
    scratch = [halves(block)] * 3 + [dma(2, N)] * 4
    return call(functools.partial(sum_kernel, ctx), [(block, jnp.float32)], scratch, 2, part)[0]


def stream_gather(own, ctx):
    scratch = [dma(ctx - 1), dma(ctx - 1)]
    outs = [((ctx,) + own.shape, own.dtype)]
    return call(functools.partial(stream_gather_kernel, ctx), outs, scratch, 5, own)[0]


def stream_sum(part, ctx):
    block = part.shape[1:]
    scratch = [pltpu.VMEM((ctx - 1,) + block, jnp.bfloat16), dma(ctx - 1), dma(ctx - 1)]
    return call(functools.partial(stream_sum_kernel, ctx), [(block, jnp.float32)], scratch, 3, part)[0]


def scatter_grads(grad_qkv, grad_out, small, part, shard, far, ctx):
    pad = padded(shard)
    cube = 2 * ctx
    total = shard * far * cube + pad - shard
    block = part.shape[1:]
    bf16 = jnp.bfloat16
    column = (far, pad, LANES)
    scratch = [
        pltpu.VMEM((total, LANES), jnp.float32),
        pltpu.VMEM((cube,) + column, bf16),
        pltpu.VMEM(column, bf16),
        pltpu.VMEM(column, bf16),
    ]
    scratch += [pltpu.VMEM((far, N, pad, LANES), bf16)] * 3 + [halves(block)] * 3
    scratch += [dma(far)] * 2 + [dma(far, N)] * 4 + [dma(2, N)] * 4
    kernel = functools.partial(grads_kernel, far, ctx, shard, pad)
    outs = [((pad, LANES), jnp.float32), (block, jnp.float32)]
    attn, out_sum = call(kernel, outs, scratch, 4, grad_qkv, grad_out, small, part)
    return attn[:shard], out_sum


def per_device(tokens, seq_lengths, attn_params, ffn_weight, out_grad):
    micro_count, rows_own = tokens.shape[0], tokens.shape[1]
    stream = rows_own * lax.axis_size("ctx")
    rows = micro_count * rows_own
    groups = HEADS // KV_HEADS
    kv_width = KV_HEADS * HEAD
    score_scale = HEAD ** (-0.5)
    units = ffn_weight.shape[1]
    far = lax.axis_size("hi")
    ctx = lax.axis_size("ctx")
    cube = 2 * ctx
    f32, bf16 = jnp.float32, jnp.bfloat16

    cot_low = out_grad.reshape(rows, D)
    ffn_all = lax.all_gather(ffn_weight.reshape(3 * units, D), "hi", axis=0, tiled=False)
    attn_rows = attn_params.reshape(-1, LANES)
    w_qkv, w_out, small, cot_all = gather_params(attn_rows, cot_low, far, ctx)
    cot_all = cot_all.reshape(-1, D)
    small = small.reshape(-1)
    b_qkv, gain_one, gain_two = small[:QKV], small[QKV : QKV + D], small[QKV + D : QKV + 2 * D]

    slot_ids = jnp.arange(stream, dtype=jnp.int32)
    first_slot = lax.axis_index("ctx") * rows_own
    own_slots = first_slot + jnp.arange(rows_own, dtype=jnp.int32)
    segment, position = jax.vmap(geometry, in_axes=(0, None))(seq_lengths[0], slot_ids)
    own_segment = lax.dynamic_slice_in_dim(segment, first_slot, rows_own, axis=1)
    own_position = lax.dynamic_slice_in_dim(position, first_slot, rows_own, axis=1)
    cosine, sine_table = rotary_tables(own_position.reshape(-1))
    cos_heads, sin_heads = cosine[:, None, :], sine_table[:, None, :]
    allowed = (own_segment[:, :, None] == segment[:, None, :]) & (
        slot_ids[None, None, :] <= own_slots[None, :, None]
    )

    x_float = tokens.reshape(rows, D).astype(f32)
    normed, norm_pull = jax.vjp(rms_norm, x_float, gain_one)
    normed_low = normed.astype(bf16)
    qkv = jnp.dot(normed_low, w_qkv, preferred_element_type=f32) + b_qkv
    query_pre, key_pre, value_pre = jnp.split(qkv, [D, D + kv_width], axis=1)
    query_low = rotate(query_pre.reshape(rows, HEADS, HEAD), cos_heads, sin_heads).astype(bf16)
    key_low = rotate(key_pre.reshape(rows, KV_HEADS, HEAD), cos_heads, sin_heads).astype(bf16)
    kv_low = jnp.concatenate([key_low.reshape(rows, kv_width), value_pre.astype(bf16)], axis=1)
    kv_all = stream_gather(kv_low, ctx).reshape(ctx, micro_count, rows_own, 2 * kv_width)
    kv_all = kv_all.transpose(1, 0, 2, 3).reshape(micro_count, stream, 2, KV_HEADS, HEAD)
    keys_all, values_all = kv_all[:, :, 0], kv_all[:, :, 1]
    query_low = query_low.reshape(micro_count, rows_own, KV_HEADS, groups, HEAD)
    scores = (
        jnp.einsum("mqkgd,mskd->mkgqs", query_low, keys_all, preferred_element_type=f32)
        * score_scale
    )
    scores = jnp.where(allowed[:, None, None], scores, -1e30)
    soft_probs = jax.nn.softmax(scores, axis=-1)
    probs_low = soft_probs.astype(bf16)
    mixed = jnp.einsum("mkgqs,mskd->mqkgd", probs_low, values_all, preferred_element_type=f32)
    mixed_low = mixed.reshape(rows, HEADS * HEAD).astype(bf16)
    second = x_float + jnp.dot(mixed_low, w_out, preferred_element_type=f32)
    normed_two, norm_two_pull = jax.vjp(rms_norm, second, gain_two)
    two_low = normed_two.astype(bf16)

    two_all = gather_rows(two_low, ctx).reshape(-1, D)
    ffn_all = ffn_all.reshape(far, 3, units, D).transpose(1, 0, 2, 3).reshape(3, far * units, D)
    w_gate, w_up, w_down = ffn_all[0], ffn_all[1], ffn_all[2]
    d_hidden = jnp.einsum("td,fd->tf", cot_all, w_down, preferred_element_type=f32)
    gate_out = jnp.einsum("td,fd->tf", two_all, w_gate, preferred_element_type=f32)
    up_out = jnp.einsum("td,fd->tf", two_all, w_up, preferred_element_type=f32)
    sig = jax.nn.sigmoid(gate_out)
    silu = gate_out * sig
    hidden_low = (silu * up_out).astype(bf16)
    gate_low = (d_hidden * up_out * sig * (1.0 + gate_out * (1.0 - sig))).astype(bf16)
    up_low = (d_hidden * silu).astype(bf16)
    d_two_part = jnp.einsum("tf,fd->td", gate_low, w_gate, preferred_element_type=f32)
    d_two_part += jnp.einsum("tf,fd->td", up_low, w_up, preferred_element_type=f32)
    d_two = sum_rows(d_two_part.astype(bf16).reshape(cube, rows, D), ctx)
    out_part = jnp.einsum("tf,fd->td", hidden_low, w_down, preferred_element_type=f32)
    grad_gate = jnp.einsum("tf,td->fd", gate_low, two_all, preferred_element_type=f32)
    grad_up = jnp.einsum("tf,td->fd", up_low, two_all, preferred_element_type=f32)
    grad_down = jnp.einsum("tf,td->fd", hidden_low, cot_all, preferred_element_type=f32)
    ffn_part = jnp.stack([grad_gate.astype(bf16), grad_up.astype(bf16), grad_down.astype(bf16)])
    ffn_part = ffn_part.reshape(3, far, units, D).transpose(1, 0, 2, 3).reshape(far, 3 * units, D)
    ffn_grad = lax.psum_scatter(ffn_part, "hi", scatter_dimension=0, tiled=False)
    ffn_grad = ffn_grad.astype(f32).reshape(3, units, D)

    d_second_part, d_gain_two = norm_two_pull(d_two)
    d_second = cot_low.astype(f32) + d_second_part
    branch_low = d_second.astype(bf16)
    d_mixed = jnp.einsum("te,de->td", branch_low, w_out, preferred_element_type=f32)
    dmix_low = d_mixed.astype(bf16).reshape(micro_count, rows_own, KV_HEADS, groups, HEAD)
    d_probs = jnp.einsum("mqkgd,mskd->mkgqs", dmix_low, values_all, preferred_element_type=f32)
    row_delta = jnp.sum(soft_probs * d_probs, axis=-1, keepdims=True)
    dscore_low = (soft_probs * (d_probs - row_delta)).astype(bf16)
    dq_rot = (
        jnp.einsum("mkgqs,mskd->mqkgd", dscore_low, keys_all, preferred_element_type=f32)
        * score_scale
    )
    dk_part = (
        jnp.einsum("mkgqs,mqkgd->mskd", dscore_low, query_low, preferred_element_type=f32)
        * score_scale
    )
    dv_part = jnp.einsum("mkgqs,mqkgd->mskd", probs_low, dmix_low, preferred_element_type=f32)
    dkv_part = jnp.concatenate(
        [
            dk_part.reshape(micro_count, stream, kv_width),
            dv_part.reshape(micro_count, stream, kv_width),
        ],
        axis=2,
    )
    dkv_part = dkv_part.astype(bf16).reshape(micro_count, ctx, rows_own, 2 * kv_width)
    dkv = stream_sum(dkv_part.transpose(1, 0, 2, 3).reshape(ctx, rows, 2 * kv_width), ctx)
    dq_low = (
        rotate_back(dq_rot.reshape(rows, HEADS, HEAD), cos_heads, sin_heads)
        .reshape(rows, HEADS * HEAD)
        .astype(bf16)
    )
    dk_rot = dkv[:, :kv_width].reshape(rows, KV_HEADS, HEAD)
    dk_low = rotate_back(dk_rot, cos_heads, sin_heads).reshape(rows, kv_width).astype(bf16)
    d_qkv = jnp.concatenate([dq_low, dk_low, dkv[:, kv_width:].astype(bf16)], axis=1)
    d_normed = jnp.einsum("te,de->td", d_qkv, w_qkv, preferred_element_type=f32)
    d_input_part, d_gain_one = norm_pull(d_normed)
    input_grad = (d_second + d_input_part).astype(bf16)
    grad_qkv = jnp.einsum("td,te->de", normed_low, d_qkv, preferred_element_type=f32)
    grad_out = jnp.einsum("td,te->de", mixed_low, branch_low, preferred_element_type=f32)
    grad_bias = jnp.sum(d_qkv.astype(f32), axis=0)
    zeros = jnp.zeros((SMALL_ROWS * LANES - QKV - 2 * D,), f32)
    small_grad = jnp.concatenate([grad_bias, d_gain_one, d_gain_two, zeros])
    attn_grad, out_sum = scatter_grads(
        grad_qkv,
        grad_out,
        small_grad.reshape(SMALL_ROWS, LANES),
        out_part.astype(bf16).reshape(cube, rows, D),
        attn_rows.shape[0],
        far,
        ctx,
    )
    result = (second + out_sum).astype(bf16)
    shape = tokens.shape
    return (result.reshape(shape), input_grad.reshape(shape), attn_grad.reshape(-1), ffn_grad)


def solution(mesh):
    grid = mesh.devices
    split = Mesh(grid.reshape(grid.shape[0] // 2, 2, grid.shape[1]), ("hi", "lo", "ctx"))
    every = ("hi", "lo", "ctx")
    return jax.shard_map(
        per_device,
        mesh=split,
        in_specs=(
            P(None, every, None),
            P(("hi", "lo"), None, None),
            P(every),
            P(None, every, None),
            P(None, every, None),
        ),
        out_specs=(
            P(None, every, None),
            P(None, every, None),
            P(every),
            P(None, every, None),
        ),
        check_vma=False,
    )
```

```python
import functools

import jax
import jax.numpy as jnp
from jax import lax
from jax.experimental import pallas as pl
from jax.experimental.pallas import tpu as pltpu
from jax.sharding import Mesh
from jax.sharding import PartitionSpec as P

D = 896
HEADS = 14
KV_HEADS = 2
HEAD = 64


EPSILON = 1e-06
THETA = 1000000.0


def rms_norm(values, gain_vec):
    return (
        values * lax.rsqrt(jnp.mean(values * values, axis=-1, keepdims=True) + EPSILON) * gain_vec
    )


def rotate_back(incoming, cosine, sine_table):
    scaled = incoming * sine_table
    half_width = incoming.shape[-1] // 2
    turned = jnp.concatenate([scaled[..., half_width:], -scaled[..., :half_width]], axis=-1)
    return incoming * cosine + turned


def geometry(seq_lens, slot_ids):
    seq_ends = jnp.cumsum(seq_lens)
    seq_starts = seq_ends - seq_lens
    filled = seq_ends[-1]
    numbers = jnp.arange(seq_lens.shape[0], dtype=jnp.int32)
    segment = jnp.sum((slot_ids[:, None] >= seq_ends[None, :]).astype(jnp.int32), axis=1)
    seq_begin = jnp.sum(
        jnp.where(segment[:, None] == numbers[None, :], seq_starts[None, :], 0), axis=1
    )
    inside = slot_ids < filled
    segment = jnp.where(inside, segment, seq_lens.shape[0] + slot_ids)
    position = jnp.where(inside, slot_ids - seq_begin, 0)
    return (segment, position)


def rotary_tables(position):
    half_width = HEAD // 2
    frequency = jnp.power(THETA, -(jnp.arange(half_width, dtype=jnp.float32) * 2.0 / HEAD))
    angles = position.astype(jnp.float32)[:, None] * frequency[None, :]
    cosine = jnp.concatenate([jnp.cos(angles), jnp.cos(angles)], axis=-1)
    sine_table = jnp.concatenate([jnp.sin(angles), jnp.sin(angles)], axis=-1)
    return (cosine, sine_table)


QKV = (HEADS + 2 * KV_HEADS) * HEAD
LANES = 128
W = D // LANES
MATRIX_ROWS = 2 * D * W + 2 * D * KV_HEADS * HEAD // LANES
SMALL_ROWS = 24
MESH = pl.DeviceIdType.MESH
NEAR = [(0, 0), (0, 1), (1, 0), (1, 1)]
N = len(NEAR)


class Place:
    def __init__(self, ctx):
        self.ctx = ctx
        self.hi = lax.axis_index("hi")
        self.lo = lax.axis_index("lo")
        self.c = lax.axis_index("ctx")
        self.sib = self.c + 1 - 2 * lax.rem(self.c, 2)

    def of(self, r, c=None):
        c = self.c if c is None else c
        a, b = NEAR[r]
        return lax.rem(self.lo + a, 2), lax.rem(c + 2 * b, self.ctx)

    def slot(self, r, c=None):
        lo, c = self.of(r, c)
        return lo * self.ctx + c

    def device(self, r):
        return (self.hi,) + self.of(r)

    def sibling(self):
        return (self.hi, self.lo, self.sib)

    def cube(self):
        return [self.device(1), self.device(2), self.sibling()]


def greet(devices):
    barrier = pltpu.get_barrier_semaphore()
    for device in devices:
        pl.semaphore_signal(barrier, inc=1, device_id=device, device_id_type=MESH)
    pl.semaphore_wait(barrier, len(devices))


def remote(src, dst, send, recv, device):
    return pltpu.make_async_remote_copy(
        src_ref=src, dst_ref=dst, send_sem=send, recv_sem=recv,
        device_id=device, device_id_type=MESH,
    )


class Unit:
    def __init__(self, at, turn, sems):
        self.at = at
        self.first, self.second = (1, 2) if turn % 2 == 0 else (2, 1)
        self.send1, self.recv1, self.send2, self.recv2 = sems
        self.started = []

    def go(self, *parts):
        copy = remote(*parts)
        copy.start()
        self.started.append(copy)

    def drain(self):
        for copy in self.started:
            copy.wait_send()


class CubeGather(Unit):
    def __init__(self, at, turn, own, aim, sems):
        super().__init__(at, turn, sems)
        self.own, self.aim = own, aim

    def push(self):
        at = self.at
        mine = self.aim(at.slot(0))
        for r in (self.first, self.second):
            self.go(self.own, mine, self.send1.at[r], self.recv1.at[r], at.device(r))
        self.go(self.own, mine, self.send2.at[0], self.recv2.at[0], at.sibling())

    def arrive(self, r, by):
        at = self.at
        here = self.aim(at.slot(r))
        remote(here, here, self.send1.at[r], self.recv1.at[r], at.device(by)).wait_recv()
        if r == self.first:
            self.go(here, here, self.send1.at[3], self.recv1.at[3], at.device(self.second))
        self.go(here, here, self.send2.at[r], self.recv2.at[r], at.sibling())

    def forward(self):
        self.arrive(self.first, self.first)
        self.arrive(self.second, self.second)

    def corner(self):
        self.arrive(3, self.second)

    def finish(self):
        at = self.at
        for r in range(N):
            here = self.aim(at.slot(r, at.sib))
            remote(here, here, self.send2.at[r], self.recv2.at[r], at.sibling()).wait_recv()
        self.drain()


class CubeScatter(Unit):
    def __init__(self, at, turn, part, bufs, sems):
        super().__init__(at, turn, sems)
        self.part = part
        self.buf1, self.tmp, self.buf2 = bufs

    def push(self):
        at = self.at
        for r in (3, self.first, self.second, 0):
            there = self.part(at.slot(r, at.sib))
            self.go(there, self.buf1.at[r], self.send1.at[r], self.recv1.at[r], at.sibling())

    def arrived(self, r):
        at, buf = self.at, self.buf1.at[r]
        remote(buf, buf, self.send1.at[r], self.recv1.at[r], at.sibling()).wait_recv()
        return self.part(at.slot(r))[...].astype(jnp.float32) + buf[...].astype(jnp.float32)

    def landed(self, r, by):
        buf = self.buf2.at[r]
        remote(buf, buf, self.send2.at[r], self.recv2.at[r], self.at.device(by)).wait_recv()
        return buf[...].astype(jnp.float32)

    def send(self, r, value, to):
        self.tmp[r] = value.astype(jnp.bfloat16)
        self.go(self.tmp.at[r], self.buf2.at[r], self.send2.at[r], self.recv2.at[r], self.at.device(to))

    def forward(self):
        self.send(3, self.arrived(3), self.first)
        self.send(self.first, self.arrived(self.first), self.first)

    def corner(self):
        value = self.arrived(self.second)
        self.send(self.second, value + self.landed(3, self.first), self.second)

    def finish(self):
        total = self.arrived(0)
        for r in (self.first, self.second):
            total = total + self.landed(r, r)
        return total


def row_units(rows):
    half = rows // 2
    return [pl.ds(u * half, half) for u in range(2)]


def row_gathers(at, own, out, sems):
    return [
        CubeGather(at, u, own.at[span], lambda slot, span=span: out.at[slot, span], [s.at[u] for s in sems])
        for u, span in enumerate(row_units(own.shape[0]))
    ]


def row_scatters(at, part, bufs, sems):
    return [
        CubeScatter(
            at, u, lambda slot, span=span: part.at[slot, span],
            [b.at[u] for b in bufs], [s.at[u] for s in sems],
        )
        for u, span in enumerate(row_units(part.shape[1]))
    ]


def params_kernel(far, ctx, shard, pad, *refs):
    attn_ref, cot_ref, qkv_ref, wout_ref, small_ref, cots_ref, held, flat = refs[:8]
    send_z, recv_z = refs[8:10]
    piece_sems, cot_sems = refs[10:14], refs[14:18]
    at = Place(ctx)
    beyond = [(lax.rem(at.hi + h, far), at.lo, at.c) for h in range(1, far)]
    greet(at.cube() + beyond)
    mine = at.slot(0)
    for h in range(1, far):
        remote(attn_ref, held.at[mine, at.hi], send_z.at[h], recv_z.at[h], beyond[h - 1]).start()
    cots = row_gathers(at, cot_ref, cots_ref, cot_sems)
    gathers = []
    for h in range(far):
        origin = lax.rem(at.hi + far - h, far)
        own = attn_ref if h == 0 else held.at[mine, origin]
        if h:
            remote(own, own, send_z.at[h], recv_z.at[h], beyond[h - 1]).wait_recv()
        gather = CubeGather(
            at, h, own, lambda slot, origin=origin: held.at[slot, origin],
            [s.at[h] for s in piece_sems],
        )
        gather.push()
        gathers.append(gather)
        if h == 0:
            held[mine, at.hi] = attn_ref[...]
            for cot in cots:
                cot.push()
            cots_ref[mine] = cot_ref[...]
    for gather in gathers:
        gather.forward()
    for gather in gathers:
        gather.corner()
    for cot in cots:
        cot.forward()
    for cot in cots:
        cot.corner()
    for gather in gathers:
        gather.finish()
    for g in range(0, far * 2 * ctx):
        block = held[g % (2 * ctx), g // (2 * ctx)].astype(jnp.float32)
        flat[pl.ds(g * shard, pad), :] = block
    for j in range(W):
        cols = pl.ds(j * LANES, LANES)
        qkv_ref[:, cols] = flat[pl.ds(j, D, stride=W), :].astype(jnp.bfloat16)
        wout_ref[:, cols] = flat[pl.ds(D * W + 2 * D + j, D, stride=W), :].astype(jnp.bfloat16)
    for j in range(2):
        cols = pl.ds(D + j * LANES, LANES)
        qkv_ref[:, cols] = flat[pl.ds(D * W + j * D, D), :].astype(jnp.bfloat16)
    small_ref[...] = flat[pl.ds(MATRIX_ROWS, SMALL_ROWS), :]
    for cot in cots:
        cot.finish()
    for h in range(1, far):
        remote(attn_ref, held.at[mine, at.hi], send_z.at[h], recv_z.at[h], beyond[h - 1]).wait_send()


def rows_kernel(ctx, own_ref, out_ref, *sems):
    at = Place(ctx)
    greet(at.cube())
    gathers = row_gathers(at, own_ref, out_ref, sems)
    for gather in gathers:
        gather.push()
    out_ref[at.slot(0)] = own_ref[...]
    for gather in gathers:
        gather.forward()
    for gather in gathers:
        gather.corner()
    for gather in gathers:
        gather.finish()


def sum_kernel(ctx, part_ref, out_ref, buf1, tmp, buf2, *sems):
    at = Place(ctx)
    greet(at.cube())
    scatters = row_scatters(at, part_ref, (buf1, tmp, buf2), sems)
    for scatter in scatters:
        scatter.push()
    for scatter in scatters:
        scatter.forward()
    for scatter in scatters:
        scatter.corner()
    for scatter, span in zip(scatters, row_units(out_ref.shape[0])):
        out_ref[span, :] = scatter.finish()
        scatter.drain()


def queries_kernel(ctx, x_ref, gain_ref, w_ref, b_ref, cos_ref, sin_ref, *refs):
    normed_ref, query_ref, kv_ref, own, send, recv = refs
    hi, lo, c = lax.axis_index("hi"), lax.axis_index("lo"), lax.axis_index("ctx")
    others = [lax.rem(c + d, ctx) for d in range(1, ctx)]
    greet([(hi, lo, other) for other in others])
    x = x_ref[...].astype(jnp.float32)
    normed = rms_norm(x, gain_ref[...]).astype(jnp.bfloat16)
    normed_ref[...] = normed
    cosine, sine = cos_ref[...], sin_ref[...]
    lane = lax.broadcasted_iota(jnp.int32, cosine.shape, 1)
    early = lax.rem(lane, HEAD) < HEAD // 2

    def tile(pre):
        ahead = pltpu.roll(pre, LANES - HEAD // 2, 1)
        behind = pltpu.roll(pre, HEAD // 2, 1)
        return pre * cosine + jnp.where(early, -ahead, behind) * sine

    kv = jnp.dot(normed, w_ref[:, D:], preferred_element_type=jnp.float32) + b_ref[:, D:]
    own[:, :LANES] = tile(kv[:, :LANES]).astype(jnp.bfloat16)
    own[:, LANES:] = kv[:, LANES:].astype(jnp.bfloat16)
    for d, other in enumerate(others):
        remote(own, kv_ref.at[c], send.at[d], recv.at[d], (hi, lo, other)).start()
    kv_ref[c] = own[...]
    query = jnp.dot(normed, w_ref[:, :D], preferred_element_type=jnp.float32) + b_ref[:, :D]
    for j in range(W):
        span = slice(j * LANES, (j + 1) * LANES)
        query_ref[:, span] = tile(query[:, span]).astype(jnp.bfloat16)
    for d, other in enumerate(others):
        here = kv_ref.at[lax.rem(c + ctx - d - 1, ctx)]
        remote(own, here, send.at[d], recv.at[d], (hi, lo, other)).wait()


def stream_sum_kernel(ctx, part_ref, out_ref, buf, send, recv):
    hi, lo, c = lax.axis_index("hi"), lax.axis_index("lo"), lax.axis_index("ctx")
    others = [lax.rem(c + d, ctx) for d in range(1, ctx)]
    greet([(hi, lo, other) for other in others])
    copies = []
    for d, other in enumerate(others):
        copy = remote(part_ref.at[other], buf.at[d], send.at[d], recv.at[d], (hi, lo, other))
        copy.start()
        copies.append(copy)
    total = part_ref[c].astype(jnp.float32)
    for d, copy in enumerate(copies):
        copy.wait()
        total = total + buf[d].astype(jnp.float32)
    out_ref[...] = total


def grads_kernel(far, ctx, shard, pad, *refs):
    qkv_ref, gout_ref, small_ref, part_ref, attn_ref, sum_ref = refs[:6]
    flat, held, low, buf3 = refs[6:10]
    attn_bufs, sum_bufs = refs[10:13], refs[13:16]
    send_z, recv_z = refs[16:18]
    attn_sems, sum_sems = refs[18:22], refs[22:26]
    at = Place(ctx)
    beyond = [(lax.rem(at.hi + h, far), at.lo, at.c) for h in range(1, far)]
    greet(at.cube() + beyond)
    sums = row_scatters(at, part_ref, sum_bufs, sum_sems)
    for unit in sums:
        unit.push()
    for j in range(W):
        cols = pl.ds(j * LANES, LANES)
        flat[pl.ds(j, D, stride=W), :] = qkv_ref[:, cols]
        flat[pl.ds(D * W + 2 * D + j, D, stride=W), :] = gout_ref[:, cols]
    for j in range(2):
        flat[pl.ds(D * W + j * D, D), :] = qkv_ref[:, pl.ds(D + j * LANES, LANES)]
    flat[pl.ds(MATRIX_ROWS, SMALL_ROWS), :] = small_ref[...]
    tail = MATRIX_ROWS + SMALL_ROWS
    flat[pl.ds(tail, flat.shape[0] - tail), :] = jnp.zeros((flat.shape[0] - tail, LANES), jnp.float32)
    for g in range(far * 2 * ctx):
        block = flat[pl.ds(g * shard, pad), :]
        held[g % (2 * ctx), g // (2 * ctx)] = block.astype(jnp.bfloat16)
    grads = []
    for h in list(range(1, far)) + [0]:
        origin = lax.rem(at.hi + h, far)
        unit = CubeScatter(
            at, h, lambda slot, origin=origin: held.at[slot, origin],
            [b.at[h] for b in attn_bufs], [s.at[h] for s in attn_sems],
        )
        unit.push()
        grads.append(unit)
    for unit in grads:
        unit.forward()
    for unit in grads:
        unit.corner()
    for unit in sums:
        unit.forward()
    crossing = []
    for h in range(1, far):
        low[h] = grads[h - 1].finish().astype(jnp.bfloat16)
        copy = remote(low.at[h], buf3.at[h], send_z.at[h], recv_z.at[h], beyond[h - 1])
        copy.start()
        crossing.append(copy)
    total = grads[far - 1].finish()
    for unit in sums:
        unit.corner()
    for unit, span in zip(sums, row_units(sum_ref.shape[0])):
        sum_ref[span, :] = unit.finish()
    for h in range(1, far):
        crossing[h - 1].wait()
        total = total + buf3[h].astype(jnp.float32)
    attn_ref[...] = total
    for unit in grads + sums:
        unit.drain()


def call(kernel, outs, scratch, number, *args):
    vmem = pl.BlockSpec(memory_space=pltpu.VMEM)
    return pl.pallas_call(
        kernel,
        out_shape=[jax.ShapeDtypeStruct(shape, kind) for shape, kind in outs],
        in_specs=[vmem] * len(args),
        out_specs=[vmem] * len(outs),
        scratch_shapes=scratch,
        compiler_params=pltpu.CompilerParams(
            collective_id=number, has_side_effects=True, vmem_limit_bytes=48 * 2**20
        ),
    )(*args)


def dma(*shape):
    return pltpu.SemaphoreType.DMA(shape)


def padded(shard):
    return -(-shard // 16) * 16


def gather_params(attn_rows, cot_low, far, ctx):
    shard = attn_rows.shape[0]
    pad = padded(shard)
    cube = 2 * ctx
    total = shard * far * cube + pad - shard
    attn_rows = jnp.pad(attn_rows, ((0, pad - shard), (0, 0)))
    bf16 = jnp.bfloat16
    outs = [
        ((D, QKV), bf16),
        ((D, D), bf16),
        ((SMALL_ROWS, LANES), jnp.float32),
        ((cube,) + cot_low.shape, bf16),
    ]
    scratch = [
        pltpu.VMEM((cube, far, pad, LANES), bf16),
        pltpu.VMEM((total, LANES), jnp.float32),
        dma(far),
        dma(far),
    ]
    scratch += [dma(far, N)] * 4 + [dma(2, N)] * 4
    kernel = functools.partial(params_kernel, far, ctx, shard, pad)
    return call(kernel, outs, scratch, 0, attn_rows, cot_low)


def gather_rows(rows_low, ctx):
    outs = [((2 * ctx,) + rows_low.shape, jnp.bfloat16)]
    return call(functools.partial(rows_kernel, ctx), outs, [dma(2, N)] * 4, 1, rows_low)[0]


def halves(block):
    return pltpu.VMEM((2, N, block[0] // 2) + block[1:], jnp.bfloat16)


def sum_rows(part, ctx):
    block = part.shape[1:]
    scratch = [halves(block)] * 3 + [dma(2, N)] * 4
    return call(functools.partial(sum_kernel, ctx), [(block, jnp.float32)], scratch, 2, part)[0]


def queries(x, gain, w_qkv, b_qkv, cosine, sine, ctx):
    rows = x.shape[0]
    kv = (rows, QKV - D)
    bf16 = jnp.bfloat16
    scratch = [pltpu.VMEM(kv, bf16), dma(ctx - 1), dma(ctx - 1)]
    outs = [((rows, D), bf16), ((rows, D), bf16), ((ctx,) + kv, bf16)]
    args = (x, gain[None], w_qkv, b_qkv[None], cosine, sine)
    return call(functools.partial(queries_kernel, ctx), outs, scratch, 5, *args)


def stream_sum(part, ctx):
    block = part.shape[1:]
    scratch = [pltpu.VMEM((ctx - 1,) + block, jnp.bfloat16), dma(ctx - 1), dma(ctx - 1)]
    return call(functools.partial(stream_sum_kernel, ctx), [(block, jnp.float32)], scratch, 3, part)[0]


def scatter_grads(grad_qkv, grad_out, small, part, shard, far, ctx):
    pad = padded(shard)
    cube = 2 * ctx
    total = shard * far * cube + pad - shard
    block = part.shape[1:]
    bf16 = jnp.bfloat16
    column = (far, pad, LANES)
    scratch = [
        pltpu.VMEM((total, LANES), jnp.float32),
        pltpu.VMEM((cube,) + column, bf16),
        pltpu.VMEM(column, bf16),
        pltpu.VMEM(column, bf16),
    ]
    scratch += [pltpu.VMEM((far, N, pad, LANES), bf16)] * 3 + [halves(block)] * 3
    scratch += [dma(far)] * 2 + [dma(far, N)] * 4 + [dma(2, N)] * 4
    kernel = functools.partial(grads_kernel, far, ctx, shard, pad)
    outs = [((pad, LANES), jnp.float32), (block, jnp.float32)]
    attn, out_sum = call(kernel, outs, scratch, 4, grad_qkv, grad_out, small, part)
    return attn[:shard], out_sum


def per_device(tokens, seq_lengths, attn_params, ffn_weight, out_grad):
    micro_count, rows_own = tokens.shape[0], tokens.shape[1]
    stream = rows_own * lax.axis_size("ctx")
    rows = micro_count * rows_own
    groups = HEADS // KV_HEADS
    kv_width = KV_HEADS * HEAD
    score_scale = HEAD ** (-0.5)
    units = ffn_weight.shape[1]
    far = lax.axis_size("hi")
    ctx = lax.axis_size("ctx")
    cube = 2 * ctx
    f32, bf16 = jnp.float32, jnp.bfloat16

    cot_low = out_grad.reshape(rows, D)
    ffn_all = lax.all_gather(ffn_weight.reshape(3 * units, D), "hi", axis=0, tiled=False)
    attn_rows = attn_params.reshape(-1, LANES)
    w_qkv, w_out, small, cot_all = gather_params(attn_rows, cot_low, far, ctx)
    cot_all = cot_all.reshape(-1, D)
    small = small.reshape(-1)
    b_qkv, gain_one, gain_two = small[:QKV], small[QKV : QKV + D], small[QKV + D : QKV + 2 * D]

    slot_ids = jnp.arange(stream, dtype=jnp.int32)
    first_slot = lax.axis_index("ctx") * rows_own
    own_slots = first_slot + jnp.arange(rows_own, dtype=jnp.int32)
    segment, position = jax.vmap(geometry, in_axes=(0, None))(seq_lengths[0], slot_ids)
    own_segment = lax.dynamic_slice_in_dim(segment, first_slot, rows_own, axis=1)
    own_position = lax.dynamic_slice_in_dim(position, first_slot, rows_own, axis=1)
    cosine, sine_table = rotary_tables(own_position.reshape(-1))
    cos_heads, sin_heads = cosine[:, None, :], sine_table[:, None, :]
    allowed = (own_segment[:, :, None] == segment[:, None, :]) & (
        slot_ids[None, None, :] <= own_slots[None, :, None]
    )

    x_float = tokens.reshape(rows, D).astype(f32)
    _, norm_pull = jax.vjp(rms_norm, x_float, gain_one)
    normed_low, query_low, kv_all = queries(
        tokens.reshape(rows, D),
        gain_one,
        w_qkv,
        b_qkv,
        jnp.concatenate([cosine, cosine], axis=-1),
        jnp.concatenate([sine_table, sine_table], axis=-1),
        ctx,
    )
    kv_all = kv_all.reshape(ctx, micro_count, rows_own, 2 * kv_width)
    kv_all = kv_all.transpose(1, 0, 2, 3).reshape(micro_count, stream, 2, KV_HEADS, HEAD)
    keys_all, values_all = kv_all[:, :, 0], kv_all[:, :, 1]
    query_low = query_low.reshape(micro_count, rows_own, KV_HEADS, groups, HEAD)
    scores = (
        jnp.einsum("mqkgd,mskd->mkgqs", query_low, keys_all, preferred_element_type=f32)
        * score_scale
    )
    scores = jnp.where(allowed[:, None, None], scores, -1e30)
    soft_probs = jax.nn.softmax(scores, axis=-1)
    probs_low = soft_probs.astype(bf16)
    mixed = jnp.einsum("mkgqs,mskd->mqkgd", probs_low, values_all, preferred_element_type=f32)
    mixed_low = mixed.reshape(rows, HEADS * HEAD).astype(bf16)
    second = x_float + jnp.dot(mixed_low, w_out, preferred_element_type=f32)
    normed_two, norm_two_pull = jax.vjp(rms_norm, second, gain_two)
    two_low = normed_two.astype(bf16)

    two_all = gather_rows(two_low, ctx).reshape(-1, D)
    ffn_all = ffn_all.reshape(far, 3, units, D).transpose(1, 0, 2, 3).reshape(3, far * units, D)
    w_gate, w_up, w_down = ffn_all[0], ffn_all[1], ffn_all[2]
    d_hidden = jnp.einsum("td,fd->tf", cot_all, w_down, preferred_element_type=f32)
    gate_out = jnp.einsum("td,fd->tf", two_all, w_gate, preferred_element_type=f32)
    up_out = jnp.einsum("td,fd->tf", two_all, w_up, preferred_element_type=f32)
    sig = jax.nn.sigmoid(gate_out)
    silu = gate_out * sig
    hidden_low = (silu * up_out).astype(bf16)
    gate_low = (d_hidden * up_out * sig * (1.0 + gate_out * (1.0 - sig))).astype(bf16)
    up_low = (d_hidden * silu).astype(bf16)
    d_two_part = jnp.einsum("tf,fd->td", gate_low, w_gate, preferred_element_type=f32)
    d_two_part += jnp.einsum("tf,fd->td", up_low, w_up, preferred_element_type=f32)
    d_two = sum_rows(d_two_part.astype(bf16).reshape(cube, rows, D), ctx)
    out_part = jnp.einsum("tf,fd->td", hidden_low, w_down, preferred_element_type=f32)
    grad_gate = jnp.einsum("tf,td->fd", gate_low, two_all, preferred_element_type=f32)
    grad_up = jnp.einsum("tf,td->fd", up_low, two_all, preferred_element_type=f32)
    grad_down = jnp.einsum("tf,td->fd", hidden_low, cot_all, preferred_element_type=f32)
    shares = [
        lax.psum_scatter(
            part.astype(bf16).reshape(far, units, D), "hi", scatter_dimension=0, tiled=False
        )
        for part in (grad_gate, grad_up, grad_down)
    ]
    ffn_grad = jnp.stack([share.astype(f32) for share in shares])

    d_second_part, d_gain_two = norm_two_pull(d_two)
    d_second = cot_low.astype(f32) + d_second_part
    branch_low = d_second.astype(bf16)
    d_mixed = jnp.einsum("te,de->td", branch_low, w_out, preferred_element_type=f32)
    dmix_low = d_mixed.astype(bf16).reshape(micro_count, rows_own, KV_HEADS, groups, HEAD)
    d_probs = jnp.einsum("mqkgd,mskd->mkgqs", dmix_low, values_all, preferred_element_type=f32)
    row_delta = jnp.sum(soft_probs * d_probs, axis=-1, keepdims=True)
    dscore_low = (soft_probs * (d_probs - row_delta)).astype(bf16)
    dq_rot = (
        jnp.einsum("mkgqs,mskd->mqkgd", dscore_low, keys_all, preferred_element_type=f32)
        * score_scale
    )
    dk_part = (
        jnp.einsum("mkgqs,mqkgd->mskd", dscore_low, query_low, preferred_element_type=f32)
        * score_scale
    )
    dv_part = jnp.einsum("mkgqs,mqkgd->mskd", probs_low, dmix_low, preferred_element_type=f32)
    dkv_part = jnp.concatenate(
        [
            dk_part.reshape(micro_count, stream, kv_width),
            dv_part.reshape(micro_count, stream, kv_width),
        ],
        axis=2,
    )
    dkv_part = dkv_part.astype(bf16).reshape(micro_count, ctx, rows_own, 2 * kv_width)
    dkv = stream_sum(dkv_part.transpose(1, 0, 2, 3).reshape(ctx, rows, 2 * kv_width), ctx)
    dq_low = (
        rotate_back(dq_rot.reshape(rows, HEADS, HEAD), cos_heads, sin_heads)
        .reshape(rows, HEADS * HEAD)
        .astype(bf16)
    )
    dk_rot = dkv[:, :kv_width].reshape(rows, KV_HEADS, HEAD)
    dk_low = rotate_back(dk_rot, cos_heads, sin_heads).reshape(rows, kv_width).astype(bf16)
    d_qkv = jnp.concatenate([dq_low, dk_low, dkv[:, kv_width:].astype(bf16)], axis=1)
    d_normed = jnp.einsum("te,de->td", d_qkv, w_qkv, preferred_element_type=f32)
    d_input_part, d_gain_one = norm_pull(d_normed)
    input_grad = (d_second + d_input_part).astype(bf16)
    grad_qkv = jnp.einsum("td,te->de", normed_low, d_qkv, preferred_element_type=f32)
    grad_out = jnp.einsum("td,te->de", mixed_low, branch_low, preferred_element_type=f32)
    grad_bias = jnp.sum(d_qkv.astype(f32), axis=0)
    zeros = jnp.zeros((SMALL_ROWS * LANES - QKV - 2 * D,), f32)
    small_grad = jnp.concatenate([grad_bias, d_gain_one, d_gain_two, zeros])
    attn_grad, out_sum = scatter_grads(
        grad_qkv,
        grad_out,
        small_grad.reshape(SMALL_ROWS, LANES),
        out_part.astype(bf16).reshape(cube, rows, D),
        attn_rows.shape[0],
        far,
        ctx,
    )
    result = (second + out_sum).astype(bf16)
    shape = tokens.shape
    return (result.reshape(shape), input_grad.reshape(shape), attn_grad.reshape(-1), ffn_grad)


def solution(mesh):
    grid = mesh.devices
    split = Mesh(grid.reshape(grid.shape[0] // 2, 2, grid.shape[1]), ("hi", "lo", "ctx"))
    every = ("hi", "lo", "ctx")
    return jax.shard_map(
        per_device,
        mesh=split,
        in_specs=(
            P(None, every, None),
            P(("hi", "lo"), None, None),
            P(every),
            P(None, every, None),
            P(None, every, None),
        ),
        out_specs=(
            P(None, every, None),
            P(None, every, None),
            P(every),
            P(None, every, None),
        ),
        check_vma=False,
    )
```

```python
import functools

import jax
import jax.numpy as jnp
from jax import lax
from jax.experimental import pallas as pl
from jax.experimental.pallas import tpu as pltpu
from jax.sharding import Mesh
from jax.sharding import PartitionSpec as P

D = 896
HEADS = 14
KV_HEADS = 2
HEAD = 64


EPSILON = 1e-06
THETA = 1000000.0


def rms_norm(values, gain_vec):
    return (
        values * lax.rsqrt(jnp.mean(values * values, axis=-1, keepdims=True) + EPSILON) * gain_vec
    )


def rotate_back(incoming, cosine, sine_table):
    scaled = incoming * sine_table
    half_width = incoming.shape[-1] // 2
    turned = jnp.concatenate([scaled[..., half_width:], -scaled[..., :half_width]], axis=-1)
    return incoming * cosine + turned


def geometry(seq_lens, slot_ids):
    seq_ends = jnp.cumsum(seq_lens)
    seq_starts = seq_ends - seq_lens
    filled = seq_ends[-1]
    numbers = jnp.arange(seq_lens.shape[0], dtype=jnp.int32)
    segment = jnp.sum((slot_ids[:, None] >= seq_ends[None, :]).astype(jnp.int32), axis=1)
    seq_begin = jnp.sum(
        jnp.where(segment[:, None] == numbers[None, :], seq_starts[None, :], 0), axis=1
    )
    inside = slot_ids < filled
    segment = jnp.where(inside, segment, seq_lens.shape[0] + slot_ids)
    position = jnp.where(inside, slot_ids - seq_begin, 0)
    return (segment, position)


def rotary_tables(position):
    half_width = HEAD // 2
    frequency = jnp.power(THETA, -(jnp.arange(half_width, dtype=jnp.float32) * 2.0 / HEAD))
    angles = position.astype(jnp.float32)[:, None] * frequency[None, :]
    cosine = jnp.concatenate([jnp.cos(angles), jnp.cos(angles)], axis=-1)
    sine_table = jnp.concatenate([jnp.sin(angles), jnp.sin(angles)], axis=-1)
    return (cosine, sine_table)


QKV = (HEADS + 2 * KV_HEADS) * HEAD
LANES = 128
W = D // LANES
MATRIX_ROWS = 2 * D * W + 2 * D * KV_HEADS * HEAD // LANES
SMALL_ROWS = 24
MESH = pl.DeviceIdType.MESH
NEAR = [(0, 0), (0, 1), (1, 0), (1, 1)]
N = len(NEAR)


class Place:
    def __init__(self, ctx):
        self.ctx = ctx
        self.hi = lax.axis_index("hi")
        self.lo = lax.axis_index("lo")
        self.c = lax.axis_index("ctx")
        self.sib = self.c + 1 - 2 * lax.rem(self.c, 2)

    def of(self, r, c=None):
        c = self.c if c is None else c
        a, b = NEAR[r]
        return lax.rem(self.lo + a, 2), lax.rem(c + 2 * b, self.ctx)

    def slot(self, r, c=None):
        lo, c = self.of(r, c)
        return lo * self.ctx + c

    def device(self, r):
        return (self.hi,) + self.of(r)

    def sibling(self):
        return (self.hi, self.lo, self.sib)

    def cube(self):
        return [self.device(1), self.device(2), self.sibling()]


def greet(devices):
    barrier = pltpu.get_barrier_semaphore()
    for device in devices:
        pl.semaphore_signal(barrier, inc=1, device_id=device, device_id_type=MESH)
    pl.semaphore_wait(barrier, len(devices))


def remote(src, dst, send, recv, device):
    return pltpu.make_async_remote_copy(
        src_ref=src, dst_ref=dst, send_sem=send, recv_sem=recv,
        device_id=device, device_id_type=MESH,
    )


class Unit:
    def __init__(self, at, turn, sems):
        self.at = at
        self.first, self.second = (1, 2) if turn % 2 == 0 else (2, 1)
        self.send1, self.recv1, self.send2, self.recv2 = sems
        self.started = []

    def go(self, *parts):
        copy = remote(*parts)
        copy.start()
        self.started.append(copy)

    def drain(self):
        for copy in self.started:
            copy.wait_send()


class CubeGather(Unit):
    def __init__(self, at, turn, own, aim, sems):
        super().__init__(at, turn, sems)
        self.own, self.aim = own, aim

    def push(self):
        at = self.at
        mine = self.aim(at.slot(0))
        for r in (self.first, self.second):
            self.go(self.own, mine, self.send1.at[r], self.recv1.at[r], at.device(r))
        self.go(self.own, mine, self.send2.at[0], self.recv2.at[0], at.sibling())

    def arrive(self, r, by):
        at = self.at
        here = self.aim(at.slot(r))
        remote(here, here, self.send1.at[r], self.recv1.at[r], at.device(by)).wait_recv()
        if r == self.first:
            self.go(here, here, self.send1.at[3], self.recv1.at[3], at.device(self.second))
        self.go(here, here, self.send2.at[r], self.recv2.at[r], at.sibling())

    def forward(self):
        self.arrive(self.first, self.first)
        self.arrive(self.second, self.second)

    def corner(self):
        self.arrive(3, self.second)

    def finish(self):
        at = self.at
        for r in range(N):
            here = self.aim(at.slot(r, at.sib))
            remote(here, here, self.send2.at[r], self.recv2.at[r], at.sibling()).wait_recv()
        self.drain()


class CubeScatter(Unit):
    def __init__(self, at, turn, part, bufs, sems):
        super().__init__(at, turn, sems)
        self.part = part
        self.buf1, self.tmp, self.buf2 = bufs

    def push(self):
        at = self.at
        for r in (3, self.first, self.second, 0):
            there = self.part(at.slot(r, at.sib))
            self.go(there, self.buf1.at[r], self.send1.at[r], self.recv1.at[r], at.sibling())

    def arrived(self, r):
        at, buf = self.at, self.buf1.at[r]
        remote(buf, buf, self.send1.at[r], self.recv1.at[r], at.sibling()).wait_recv()
        return self.part(at.slot(r))[...].astype(jnp.float32) + buf[...].astype(jnp.float32)

    def landed(self, r, by):
        buf = self.buf2.at[r]
        remote(buf, buf, self.send2.at[r], self.recv2.at[r], self.at.device(by)).wait_recv()
        return buf[...].astype(jnp.float32)

    def send(self, r, value, to):
        self.tmp[r] = value.astype(jnp.bfloat16)
        self.go(self.tmp.at[r], self.buf2.at[r], self.send2.at[r], self.recv2.at[r], self.at.device(to))

    def forward(self):
        self.send(3, self.arrived(3), self.first)
        self.send(self.first, self.arrived(self.first), self.first)

    def corner(self):
        value = self.arrived(self.second)
        self.send(self.second, value + self.landed(3, self.first), self.second)

    def finish(self):
        total = self.arrived(0)
        for r in (self.first, self.second):
            total = total + self.landed(r, r)
        return total


def row_units(rows):
    half = rows // 2
    return [pl.ds(u * half, half) for u in range(2)]


def row_gathers(at, own, out, sems):
    return [
        CubeGather(at, u, own.at[span], lambda slot, span=span: out.at[slot, span], [s.at[u] for s in sems])
        for u, span in enumerate(row_units(own.shape[0]))
    ]


def row_scatters(at, part, bufs, sems):
    return [
        CubeScatter(
            at, u, lambda slot, span=span: part.at[slot, span],
            [b.at[u] for b in bufs], [s.at[u] for s in sems],
        )
        for u, span in enumerate(row_units(part.shape[1]))
    ]


def params_kernel(far, ctx, shard, pad, *refs):
    attn_ref, cot_ref, qkv_ref, wout_ref, small_ref, cots_ref, held, flat = refs[:8]
    send_z, recv_z = refs[8:10]
    piece_sems, cot_sems = refs[10:14], refs[14:18]
    at = Place(ctx)
    beyond = [(lax.rem(at.hi + h, far), at.lo, at.c) for h in range(1, far)]
    greet(at.cube() + beyond)
    mine = at.slot(0)
    for h in range(1, far):
        remote(attn_ref, held.at[mine, at.hi], send_z.at[h], recv_z.at[h], beyond[h - 1]).start()
    cots = row_gathers(at, cot_ref, cots_ref, cot_sems)
    gathers = []
    for h in range(far):
        origin = lax.rem(at.hi + far - h, far)
        own = attn_ref if h == 0 else held.at[mine, origin]
        if h:
            remote(own, own, send_z.at[h], recv_z.at[h], beyond[h - 1]).wait_recv()
        gather = CubeGather(
            at, h, own, lambda slot, origin=origin: held.at[slot, origin],
            [s.at[h] for s in piece_sems],
        )
        gather.push()
        gathers.append(gather)
        if h == 0:
            held[mine, at.hi] = attn_ref[...]
            for cot in cots:
                cot.push()
            cots_ref[mine] = cot_ref[...]
    for gather in gathers:
        gather.forward()
    for gather in gathers:
        gather.corner()
    for cot in cots:
        cot.forward()
    for cot in cots:
        cot.corner()
    for gather in gathers:
        gather.finish()
    for g in range(0, far * 2 * ctx):
        block = held[g % (2 * ctx), g // (2 * ctx)].astype(jnp.float32)
        flat[pl.ds(g * shard, pad), :] = block
    for j in range(W):
        cols = pl.ds(j * LANES, LANES)
        qkv_ref[:, cols] = flat[pl.ds(j, D, stride=W), :].astype(jnp.bfloat16)
        wout_ref[:, cols] = flat[pl.ds(D * W + 2 * D + j, D, stride=W), :].astype(jnp.bfloat16)
    for j in range(2):
        cols = pl.ds(D + j * LANES, LANES)
        qkv_ref[:, cols] = flat[pl.ds(D * W + j * D, D), :].astype(jnp.bfloat16)
    small_ref[...] = flat[pl.ds(MATRIX_ROWS, SMALL_ROWS), :]
    for cot in cots:
        cot.finish()
    for h in range(1, far):
        remote(attn_ref, held.at[mine, at.hi], send_z.at[h], recv_z.at[h], beyond[h - 1]).wait_send()


def rows_kernel(ctx, own_ref, out_ref, *sems):
    at = Place(ctx)
    greet(at.cube())
    gathers = row_gathers(at, own_ref, out_ref, sems)
    for gather in gathers:
        gather.push()
    out_ref[at.slot(0)] = own_ref[...]
    for gather in gathers:
        gather.forward()
    for gather in gathers:
        gather.corner()
    for gather in gathers:
        gather.finish()


def sum_kernel(ctx, part_ref, out_ref, buf1, tmp, buf2, *sems):
    at = Place(ctx)
    greet(at.cube())
    scatters = row_scatters(at, part_ref, (buf1, tmp, buf2), sems)
    for scatter in scatters:
        scatter.push()
    for scatter in scatters:
        scatter.forward()
    for scatter in scatters:
        scatter.corner()
    for scatter, span in zip(scatters, row_units(out_ref.shape[0])):
        out_ref[span, :] = scatter.finish()
        scatter.drain()


def queries_kernel(ctx, x_ref, gain_ref, w_ref, b_ref, cos_ref, sin_ref, *refs):
    normed_ref, query_ref, kv_ref, own, send, recv = refs
    hi, lo, c = lax.axis_index("hi"), lax.axis_index("lo"), lax.axis_index("ctx")
    others = [lax.rem(c + d, ctx) for d in range(1, ctx)]
    greet([(hi, lo, other) for other in others])
    x = x_ref[...].astype(jnp.float32)
    normed = rms_norm(x, gain_ref[...]).astype(jnp.bfloat16)
    normed_ref[...] = normed
    cosine, sine = cos_ref[...], sin_ref[...]
    lane = lax.broadcasted_iota(jnp.int32, cosine.shape, 1)
    early = lax.rem(lane, HEAD) < HEAD // 2

    def tile(pre):
        ahead = pltpu.roll(pre, LANES - HEAD // 2, 1)
        behind = pltpu.roll(pre, HEAD // 2, 1)
        return pre * cosine + jnp.where(early, -ahead, behind) * sine

    kv = jnp.dot(normed, w_ref[:, D:], preferred_element_type=jnp.float32) + b_ref[:, D:]
    own[:, :LANES] = tile(kv[:, :LANES]).astype(jnp.bfloat16)
    own[:, LANES:] = kv[:, LANES:].astype(jnp.bfloat16)
    for d, other in enumerate(others):
        remote(own, kv_ref.at[c], send.at[d], recv.at[d], (hi, lo, other)).start()
    kv_ref[c] = own[...]
    query = jnp.dot(normed, w_ref[:, :D], preferred_element_type=jnp.float32) + b_ref[:, :D]
    for j in range(W):
        span = slice(j * LANES, (j + 1) * LANES)
        query_ref[:, span] = tile(query[:, span]).astype(jnp.bfloat16)
    for d, other in enumerate(others):
        here = kv_ref.at[lax.rem(c + ctx - d - 1, ctx)]
        remote(own, here, send.at[d], recv.at[d], (hi, lo, other)).wait()


def stream_sum_kernel(ctx, part_ref, out_ref, buf, send, recv):
    hi, lo, c = lax.axis_index("hi"), lax.axis_index("lo"), lax.axis_index("ctx")
    others = [lax.rem(c + d, ctx) for d in range(1, ctx)]
    greet([(hi, lo, other) for other in others])
    copies = []
    for d, other in enumerate(others):
        copy = remote(part_ref.at[other], buf.at[d], send.at[d], recv.at[d], (hi, lo, other))
        copy.start()
        copies.append(copy)
    total = part_ref[c].astype(jnp.float32)
    for d, copy in enumerate(copies):
        copy.wait()
        total = total + buf[d].astype(jnp.float32)
    out_ref[...] = total


def grads_kernel(far, ctx, shard, pad, *refs):
    qkv_ref, gout_ref, small_ref, part_ref, attn_ref, sum_ref = refs[:6]
    flat, held, low, buf3 = refs[6:10]
    attn_bufs, sum_bufs = refs[10:13], refs[13:16]
    send_z, recv_z = refs[16:18]
    attn_sems, sum_sems = refs[18:22], refs[22:26]
    at = Place(ctx)
    beyond = [(lax.rem(at.hi + h, far), at.lo, at.c) for h in range(1, far)]
    greet(at.cube() + beyond)
    sums = row_scatters(at, part_ref, sum_bufs, sum_sems)
    for unit in sums:
        unit.push()
    for j in range(W):
        cols = pl.ds(j * LANES, LANES)
        flat[pl.ds(j, D, stride=W), :] = qkv_ref[:, cols]
        flat[pl.ds(D * W + 2 * D + j, D, stride=W), :] = gout_ref[:, cols]
    for j in range(2):
        flat[pl.ds(D * W + j * D, D), :] = qkv_ref[:, pl.ds(D + j * LANES, LANES)]
    flat[pl.ds(MATRIX_ROWS, SMALL_ROWS), :] = small_ref[...]
    tail = MATRIX_ROWS + SMALL_ROWS
    flat[pl.ds(tail, flat.shape[0] - tail), :] = jnp.zeros((flat.shape[0] - tail, LANES), jnp.float32)
    for g in range(far * 2 * ctx):
        block = flat[pl.ds(g * shard, pad), :]
        held[g % (2 * ctx), g // (2 * ctx)] = block.astype(jnp.bfloat16)
    grads = []
    for h in list(range(1, far)) + [0]:
        origin = lax.rem(at.hi + h, far)
        unit = CubeScatter(
            at, h, lambda slot, origin=origin: held.at[slot, origin],
            [b.at[h] for b in attn_bufs], [s.at[h] for s in attn_sems],
        )
        unit.push()
        grads.append(unit)
    for unit in grads:
        unit.forward()
    for unit in grads:
        unit.corner()
    for unit in sums:
        unit.forward()
    crossing = []
    for h in range(1, far):
        low[h] = grads[h - 1].finish().astype(jnp.bfloat16)
        copy = remote(low.at[h], buf3.at[h], send_z.at[h], recv_z.at[h], beyond[h - 1])
        copy.start()
        crossing.append(copy)
    total = grads[far - 1].finish()
    for unit in sums:
        unit.corner()
    for unit, span in zip(sums, row_units(sum_ref.shape[0])):
        sum_ref[span, :] = unit.finish()
    for h in range(1, far):
        crossing[h - 1].wait()
        total = total + buf3[h].astype(jnp.float32)
    attn_ref[...] = total
    for unit in grads + sums:
        unit.drain()


def call(kernel, outs, scratch, number, *args):
    vmem = pl.BlockSpec(memory_space=pltpu.VMEM)
    return pl.pallas_call(
        kernel,
        out_shape=[jax.ShapeDtypeStruct(shape, kind) for shape, kind in outs],
        in_specs=[vmem] * len(args),
        out_specs=[vmem] * len(outs),
        scratch_shapes=scratch,
        compiler_params=pltpu.CompilerParams(
            collective_id=number, has_side_effects=True, vmem_limit_bytes=48 * 2**20
        ),
    )(*args)


def dma(*shape):
    return pltpu.SemaphoreType.DMA(shape)


def padded(shard):
    return -(-shard // 16) * 16


def gather_params(attn_rows, cot_low, far, ctx):
    shard = attn_rows.shape[0]
    pad = padded(shard)
    cube = 2 * ctx
    total = shard * far * cube + pad - shard
    attn_rows = jnp.pad(attn_rows, ((0, pad - shard), (0, 0)))
    bf16 = jnp.bfloat16
    outs = [
        ((D, QKV), bf16),
        ((D, D), bf16),
        ((SMALL_ROWS, LANES), jnp.float32),
        ((cube,) + cot_low.shape, bf16),
    ]
    scratch = [
        pltpu.VMEM((cube, far, pad, LANES), bf16),
        pltpu.VMEM((total, LANES), jnp.float32),
        dma(far),
        dma(far),
    ]
    scratch += [dma(far, N)] * 4 + [dma(2, N)] * 4
    kernel = functools.partial(params_kernel, far, ctx, shard, pad)
    return call(kernel, outs, scratch, 0, attn_rows, cot_low)


def gather_rows(rows_low, ctx):
    outs = [((2 * ctx,) + rows_low.shape, jnp.bfloat16)]
    return call(functools.partial(rows_kernel, ctx), outs, [dma(2, N)] * 4, 1, rows_low)[0]


def halves(block):
    return pltpu.VMEM((2, N, block[0] // 2) + block[1:], jnp.bfloat16)


def sum_rows(part, ctx):
    block = part.shape[1:]
    scratch = [halves(block)] * 3 + [dma(2, N)] * 4
    return call(functools.partial(sum_kernel, ctx), [(block, jnp.float32)], scratch, 2, part)[0]


def queries(x, gain, w_qkv, b_qkv, cosine, sine, ctx):
    rows = x.shape[0]
    kv = (rows, QKV - D)
    bf16 = jnp.bfloat16
    scratch = [pltpu.VMEM(kv, bf16), dma(ctx - 1), dma(ctx - 1)]
    outs = [((rows, D), bf16), ((rows, D), bf16), ((ctx,) + kv, bf16)]
    args = (x, gain[None], w_qkv, b_qkv[None], cosine, sine)
    return call(functools.partial(queries_kernel, ctx), outs, scratch, 5, *args)


def stream_sum(part, ctx):
    block = part.shape[1:]
    scratch = [pltpu.VMEM((ctx - 1,) + block, jnp.bfloat16), dma(ctx - 1), dma(ctx - 1)]
    return call(functools.partial(stream_sum_kernel, ctx), [(block, jnp.float32)], scratch, 3, part)[0]


def scatter_grads(grad_qkv, grad_out, small, part, shard, far, ctx):
    pad = padded(shard)
    cube = 2 * ctx
    total = shard * far * cube + pad - shard
    block = part.shape[1:]
    bf16 = jnp.bfloat16
    column = (far, pad, LANES)
    scratch = [
        pltpu.VMEM((total, LANES), jnp.float32),
        pltpu.VMEM((cube,) + column, bf16),
        pltpu.VMEM(column, bf16),
        pltpu.VMEM(column, bf16),
    ]
    scratch += [pltpu.VMEM((far, N, pad, LANES), bf16)] * 3 + [halves(block)] * 3
    scratch += [dma(far)] * 2 + [dma(far, N)] * 4 + [dma(2, N)] * 4
    kernel = functools.partial(grads_kernel, far, ctx, shard, pad)
    outs = [((pad, LANES), jnp.float32), (block, jnp.float32)]
    attn, out_sum = call(kernel, outs, scratch, 4, grad_qkv, grad_out, small, part)
    return attn[:shard], out_sum


def per_device(tokens, seq_lengths, attn_params, ffn_weight, out_grad):
    micro_count, rows_own = tokens.shape[0], tokens.shape[1]
    stream = rows_own * lax.axis_size("ctx")
    rows = micro_count * rows_own
    groups = HEADS // KV_HEADS
    kv_width = KV_HEADS * HEAD
    score_scale = HEAD ** (-0.5)
    units = ffn_weight.shape[1]
    far = lax.axis_size("hi")
    ctx = lax.axis_size("ctx")
    cube = 2 * ctx
    f32, bf16 = jnp.float32, jnp.bfloat16

    cot_low = out_grad.reshape(rows, D)
    ffn_all = lax.all_gather(ffn_weight.reshape(3 * units, D), "hi", axis=0, tiled=False)
    attn_rows = attn_params.reshape(-1, LANES)
    w_qkv, w_out, small, cot_all = gather_params(attn_rows, cot_low, far, ctx)
    cot_all = cot_all.reshape(-1, D)
    small = small.reshape(-1)
    b_qkv, gain_one, gain_two = small[:QKV], small[QKV : QKV + D], small[QKV + D : QKV + 2 * D]

    slot_ids = jnp.arange(stream, dtype=jnp.int32)
    first_slot = lax.axis_index("ctx") * rows_own
    own_slots = first_slot + jnp.arange(rows_own, dtype=jnp.int32)
    segment, position = jax.vmap(geometry, in_axes=(0, None))(seq_lengths[0], slot_ids)
    own_segment = lax.dynamic_slice_in_dim(segment, first_slot, rows_own, axis=1)
    own_position = lax.dynamic_slice_in_dim(position, first_slot, rows_own, axis=1)
    cosine, sine_table = rotary_tables(own_position.reshape(-1))
    cos_heads, sin_heads = cosine[:, None, :], sine_table[:, None, :]
    allowed = (own_segment[:, :, None] == segment[:, None, :]) & (
        slot_ids[None, None, :] <= own_slots[None, :, None]
    )

    x_float = tokens.reshape(rows, D).astype(f32)
    _, norm_pull = jax.vjp(rms_norm, x_float, gain_one)
    normed_low, query_low, kv_all = queries(
        tokens.reshape(rows, D),
        gain_one,
        w_qkv,
        b_qkv,
        jnp.concatenate([cosine, cosine], axis=-1),
        jnp.concatenate([sine_table, sine_table], axis=-1),
        ctx,
    )
    kv_all = kv_all.reshape(ctx, micro_count, rows_own, 2 * kv_width)
    kv_all = kv_all.transpose(1, 0, 2, 3).reshape(micro_count, stream, 2, KV_HEADS, HEAD)
    keys_all, values_all = kv_all[:, :, 0], kv_all[:, :, 1]
    query_low = query_low.reshape(micro_count, rows_own, KV_HEADS, groups, HEAD)
    scores = (
        jnp.einsum("mqkgd,mskd->mkgqs", query_low, keys_all, preferred_element_type=f32)
        * score_scale
    )
    scores = jnp.where(allowed[:, None, None], scores, -1e30)
    soft_probs = jax.nn.softmax(scores, axis=-1)
    probs_low = soft_probs.astype(bf16)
    mixed = jnp.einsum("mkgqs,mskd->mqkgd", probs_low, values_all, preferred_element_type=f32)
    mixed_low = mixed.reshape(rows, HEADS * HEAD).astype(bf16)
    second = x_float + jnp.dot(mixed_low, w_out, preferred_element_type=f32)
    normed_two, norm_two_pull = jax.vjp(rms_norm, second, gain_two)
    two_low = normed_two.astype(bf16)

    two_all = gather_rows(two_low, ctx).reshape(-1, D)
    ffn_all = ffn_all.reshape(far, 3, units, D).transpose(1, 0, 2, 3).reshape(3, far * units, D)
    w_gate, w_up, w_down = ffn_all[0], ffn_all[1], ffn_all[2]
    d_hidden = jnp.einsum("td,fd->tf", cot_all, w_down, preferred_element_type=f32)
    gate_out = jnp.einsum("td,fd->tf", two_all, w_gate, preferred_element_type=f32)
    up_out = jnp.einsum("td,fd->tf", two_all, w_up, preferred_element_type=f32)
    sig = jax.nn.sigmoid(gate_out)
    silu = gate_out * sig
    hidden_low = (silu * up_out).astype(bf16)
    gate_low = (d_hidden * up_out * sig * (1.0 + gate_out * (1.0 - sig))).astype(bf16)
    up_low = (d_hidden * silu).astype(bf16)
    d_two_part = jnp.einsum("tf,fd->td", gate_low, w_gate, preferred_element_type=f32)
    d_two_part += jnp.einsum("tf,fd->td", up_low, w_up, preferred_element_type=f32)
    d_two = sum_rows(d_two_part.astype(bf16).reshape(cube, rows, D), ctx)
    out_part = jnp.einsum("tf,fd->td", hidden_low, w_down, preferred_element_type=f32)
    grad_gate = jnp.einsum("tf,td->fd", gate_low, two_all, preferred_element_type=f32)
    grad_up = jnp.einsum("tf,td->fd", up_low, two_all, preferred_element_type=f32)
    grad_down = jnp.einsum("tf,td->fd", hidden_low, cot_all, preferred_element_type=f32)
    ffn_part = jnp.stack([grad_gate.astype(bf16), grad_up.astype(bf16), grad_down.astype(bf16)])
    ffn_part = ffn_part.reshape(3, far, units, D).transpose(1, 0, 2, 3).reshape(far, 3 * units, D)
    ffn_grad = lax.psum_scatter(ffn_part, "hi", scatter_dimension=0, tiled=False)
    ffn_grad = ffn_grad.astype(f32).reshape(3, units, D)

    d_second_part, d_gain_two = norm_two_pull(d_two)
    d_second = cot_low.astype(f32) + d_second_part
    branch_low = d_second.astype(bf16)
    d_mixed = jnp.einsum("te,de->td", branch_low, w_out, preferred_element_type=f32)
    dmix_low = d_mixed.astype(bf16).reshape(micro_count, rows_own, KV_HEADS, groups, HEAD)
    d_probs = jnp.einsum("mqkgd,mskd->mkgqs", dmix_low, values_all, preferred_element_type=f32)
    row_delta = jnp.sum(soft_probs * d_probs, axis=-1, keepdims=True)
    dscore_low = (soft_probs * (d_probs - row_delta)).astype(bf16)
    dq_rot = (
        jnp.einsum("mkgqs,mskd->mqkgd", dscore_low, keys_all, preferred_element_type=f32)
        * score_scale
    )
    dk_part = (
        jnp.einsum("mkgqs,mqkgd->mskd", dscore_low, query_low, preferred_element_type=f32)
        * score_scale
    )
    dv_part = jnp.einsum("mkgqs,mqkgd->mskd", probs_low, dmix_low, preferred_element_type=f32)
    dkv_part = jnp.concatenate(
        [
            dk_part.reshape(micro_count, stream, kv_width),
            dv_part.reshape(micro_count, stream, kv_width),
        ],
        axis=2,
    )
    dkv_part = dkv_part.astype(bf16).reshape(micro_count, ctx, rows_own, 2 * kv_width)
    dkv = stream_sum(dkv_part.transpose(1, 0, 2, 3).reshape(ctx, rows, 2 * kv_width), ctx)
    dq_low = (
        rotate_back(dq_rot.reshape(rows, HEADS, HEAD), cos_heads, sin_heads)
        .reshape(rows, HEADS * HEAD)
        .astype(bf16)
    )
    dk_rot = dkv[:, :kv_width].reshape(rows, KV_HEADS, HEAD)
    dk_low = rotate_back(dk_rot, cos_heads, sin_heads).reshape(rows, kv_width).astype(bf16)
    d_qkv = jnp.concatenate([dq_low, dk_low, dkv[:, kv_width:].astype(bf16)], axis=1)
    d_normed = jnp.einsum("te,de->td", d_qkv, w_qkv, preferred_element_type=f32)
    d_input_part, d_gain_one = norm_pull(d_normed)
    input_grad = (d_second + d_input_part).astype(bf16)
    grad_qkv = jnp.einsum("td,te->de", normed_low, d_qkv, preferred_element_type=f32)
    grad_out = jnp.einsum("td,te->de", mixed_low, branch_low, preferred_element_type=f32)
    grad_bias = jnp.sum(d_qkv.astype(f32), axis=0)
    zeros = jnp.zeros((SMALL_ROWS * LANES - QKV - 2 * D,), f32)
    small_grad = jnp.concatenate([grad_bias, d_gain_one, d_gain_two, zeros])
    attn_grad, out_sum = scatter_grads(
        grad_qkv,
        grad_out,
        small_grad.reshape(SMALL_ROWS, LANES),
        out_part.astype(bf16).reshape(cube, rows, D),
        attn_rows.shape[0],
        far,
        ctx,
    )
    result = (second + out_sum).astype(bf16)
    shape = tokens.shape
    return (result.reshape(shape), input_grad.reshape(shape), attn_grad.reshape(-1), ffn_grad)


def solution(mesh):
    grid = mesh.devices
    split = Mesh(grid.reshape(grid.shape[0] // 2, 2, grid.shape[1]), ("hi", "lo", "ctx"))
    every = ("hi", "lo", "ctx")
    return jax.shard_map(
        per_device,
        mesh=split,
        in_specs=(
            P(None, every, None),
            P(("hi", "lo"), None, None),
            P(every),
            P(None, every, None),
            P(None, every, None),
        ),
        out_specs=(
            P(None, every, None),
            P(None, every, None),
            P(every),
            P(None, every, None),
        ),
        check_vma=False,
    )
```
